32 devices in a mesh: cfg: 2 (over y), space: 8 (over z, x), tm: 2 (over core).
Axes of the slice: x: 2, y: 2, z: 4, core: 2. Of those that a mesh axis runs over, the one named last changes fastest.
Arguments:
- solutions: float32 [4, 4, 2, 3, 8, 2048], P(('cfg', 'tm'), None, None, None, 'space'), parts along dimension 0, may hold values from -16 to 16
- links: float32 [4, 3, 2, 3, 3, 8, 2048], P(('cfg', 'tm'), None, None, None, None, 'space'), parts along dimension 0, may hold values from -0.75 to 1.75
- eigvecs: bfloat16 [4, 128, 2, 3, 8, 2048], P(('cfg', 'tm'), 'space'), parts along dimension 0, may hold values from -0.01953125 to 0.01953125
Outputs:
- smeared: bfloat16 [4, 4, 2, 3, 8, 2048], P(('cfg', 'tm'), None, None, None, 'space'), parts along dimension 0
- coefficients: float32 [4, 128, 8], P(('cfg', 'tm'), 'space'), parts along dimension 0
The draws below stay inside these ranges and needn't reach their ends.
There are 2 independent parts, one for each index of `cfg`. The reference program is written for one: setup_inputs(seed, part) draws one part's arguments, and reference() takes and returns one part's arrays. A program takes and returns all parts, laid end to end along the dimension named above; each array names one. Nothing has to cross between parts.
All inputs are finite; a program needn't handle non-finite values.
Results may differ from the reference program's by a relative error of at most 0.0045.
Values may be sent and summed in bfloat16 or wider, within the bound.
No kernel may reach another device: no remote copies, remote signals or barrier semaphores. Data moves between devices by JAX's collectives and lax.ppermute only.
A program may use at most 192 MiB of HBM per device.

```python
import jax
import jax.numpy as jnp
from jax import lax

K = 128
NVEC = 4
NSMEAR = 4
LX = 64
LY = 64
NT = 2
ZF = 4
ROWS = 8
COLS = 2048


def draw_links(key, part):
    key = jax.random.fold_in(key, 11)
    shape = (NT, 3, 2, 3, 3, ROWS, COLS)
    noise = 0.25 * jax.random.truncated_normal(key, -3.0, 3.0, shape, jnp.float32)
    rows = lax.broadcasted_iota(jnp.int32, shape, 3)
    columns = lax.broadcasted_iota(jnp.int32, shape, 4)
    halves = lax.broadcasted_iota(jnp.int32, shape, 2)
    unit = jnp.where((rows == columns) & (halves == 0), 1.0, 0.0).astype(jnp.float32)
    return noise + unit


def block_levels(key, dims, cuts, smallest, top_value):
    def one(dim, parts):
        steps = jax.random.uniform(jax.random.fold_in(jax.random.fold_in(key, 6), dim), (parts,), jnp.float32, smallest / len(cuts), top_value / len(cuts))
        return jnp.repeat(jnp.exp(steps), dims[dim] // parts).reshape((-1,) + (1,) * (len(dims) - dim - 1))

    level = one(*cuts[0])
    for cut in cuts[1:]:
        level = level * one(*cut)
    return level


def gaussian(key, dims, deviation, bound, shards=(), dtype=jnp.bfloat16):
    factor_of = block_levels(key, dims, shards, -0.22, 0.18) if shards else 1.0
    result = jax.random.normal(key, dims, jnp.float32) * deviation * factor_of
    return jnp.minimum(jnp.maximum(result, -bound), bound).astype(dtype)


def setup_inputs(seed: int = 0, part: int = 0) -> dict:
    splits = jax.random.split(jax.random.key(seed), 4)
    own_keys = jax.random.split(jax.random.fold_in(splits[3], part), 4)
    solutions = gaussian(own_keys[0], (NT, NVEC, 2, 3, ROWS, COLS), 4.0, 16.0, ((0, 2), (4, 8)), jnp.float32)
    links = draw_links(jax.random.fold_in(jax.random.fold_in(splits[3], part), 71), part)
    eigvecs = gaussian(own_keys[2], (NT, K, 2, 3, ROWS, COLS), (6 * ZF * LX * LY) ** -0.5, 0.01953125, ((0, 2), (1, 8)))
    return {"solutions": solutions, "links": links, "eigvecs": eigvecs}


kappa_hop = 0.1


def color_product(link_real, link_imag, field_real, field_imag):
    link_real = link_real[:, None]
    link_imag = link_imag[:, None]
    field_real = field_real[:, :, None]
    field_imag = field_imag[:, :, None]
    out_real = jnp.sum(link_real * field_real - link_imag * field_imag, axis=3)
    out_imag = jnp.sum(link_real * field_imag + link_imag * field_real, axis=3)
    return out_real, out_imag


def adjoint_product(link_real, link_imag, field_real, field_imag):
    return color_product(jnp.swapaxes(link_real, 1, 2), -jnp.swapaxes(link_imag, 1, 2), field_real, field_imag)


def to_grid(field):
    return field.reshape(field.shape[:-2] + (ZF, LY, LX))


def from_grid(field):
    return field.reshape(field.shape[:-3] + (2 * ZF, LX * LY // 2))


def hopping(real, imag, link_grid):
    total_real = jnp.zeros_like(real)
    total_imag = jnp.zeros_like(imag)
    for along in range(3):
        axis_index = real.ndim - 1 - along
        link_real = link_grid[:, along, 0]
        link_imag = link_grid[:, along, 1]
        ahead_real, ahead_imag = color_product(link_real, link_imag, jnp.roll(real, -1, axis_index), jnp.roll(imag, -1, axis_index))
        back_real, back_imag = adjoint_product(link_real, link_imag, real, imag)
        total_real = total_real + ahead_real + jnp.roll(back_real, 1, axis_index)
        total_imag = total_imag + ahead_imag + jnp.roll(back_imag, 1, axis_index)
    return total_real, total_imag


def reference(solutions, links, eigvecs):
    real = to_grid(solutions[:, :, 0])
    imag = to_grid(solutions[:, :, 1])
    link_grid = to_grid(links)
    for step in range(NSMEAR):
        hop_real, hop_imag = hopping(real, imag, link_grid)
        real = real + kappa_hop * (hop_real - 6.0 * real)
        imag = imag + kappa_hop * (hop_imag - 6.0 * imag)
    smeared = jnp.stack([from_grid(real), from_grid(imag)], axis=2).astype(jnp.bfloat16)
    swapped = jnp.stack([smeared[:, :, 1], -smeared[:, :, 0]], axis=2)
    paired = jnp.concatenate([smeared, swapped], axis=1)

    def project(operands):
        left = operands[0].reshape(K, -1)
        right = operands[1].reshape(2 * NVEC, -1)
        return jnp.dot(left, right.T, preferred_element_type=jnp.float32)

    coefficients = lax.map(project, (eigvecs, paired))
    return smeared, coefficients
```

```python
import jax
import jax.numpy as jnp
import numpy as np
from jax import lax
from jax.experimental import pallas as pl
from jax.experimental.pallas import tpu as pltpu
from jax.sharding import PartitionSpec as P

NSMEAR = 4
LX = 64


kappa_hop = 0.1


def swapped_2(block, axis, stride):
    count = lax.axis_size(axis)
    route = []
    for low in range(count):
        high = low | 1 << stride
        if high != low and high < count:
            route += [(low, high), (high, low)]
    return lax.ppermute(block, axis, route)


def for_sending(array):

    def short(part):
        return part.astype(jnp.bfloat16) if part.dtype == jnp.float32 else part

    return jax.tree.map(short, array)


def from_behind(block, axis, distance):
    devices = range(lax.axis_size(axis))
    route = [((i - distance) % len(devices), i) for i in devices]
    return lax.ppermute(block, axis, route)


def color_product(link_real, link_imag, field_real, field_imag):
    out_real = None
    out_imag = None
    for inner in range(3):
        column_real = link_real[:, None, :, inner]
        column_imag = link_imag[:, None, :, inner]
        entry_real = field_real[:, :, inner : inner + 1]
        entry_imag = field_imag[:, :, inner : inner + 1]
        term_real = column_real * entry_real - column_imag * entry_imag
        term_imag = column_real * entry_imag + column_imag * entry_real
        if out_real is None:
            out_real = term_real
            out_imag = term_imag
        else:
            out_real = out_real + term_real
            out_imag = out_imag + term_imag
    return (out_real, out_imag)


def adjoint_product(link_real, link_imag, field_real, field_imag):
    return color_product(
        jnp.swapaxes(link_real, 1, 2), -jnp.swapaxes(link_imag, 1, 2), field_real, field_imag
    )


def hopping(real, imag, link_flat):
    sites = real.shape[-1]
    x_place = lax.broadcasted_iota(jnp.int32, (sites,), 0) % LX
    at_end = x_place == LX - 1
    at_start = x_place == 0
    link_real = link_flat[:, 0, 0]
    link_imag = link_flat[:, 0, 1]
    next_real = jnp.where(at_end, jnp.roll(real, LX - 1, 3), jnp.roll(real, -1, 3))
    next_imag = jnp.where(at_end, jnp.roll(imag, LX - 1, 3), jnp.roll(imag, -1, 3))
    ahead_real, ahead_imag = color_product(link_real, link_imag, next_real, next_imag)
    back_real, back_imag = adjoint_product(link_real, link_imag, real, imag)
    total_real = ahead_real + jnp.where(
        at_start, jnp.roll(back_real, 1 - LX, 3), jnp.roll(back_real, 1, 3)
    )
    total_imag = ahead_imag + jnp.where(
        at_start, jnp.roll(back_imag, 1 - LX, 3), jnp.roll(back_imag, 1, 3)
    )
    link_real = link_flat[:, 1, 0]
    link_imag = link_flat[:, 1, 1]
    back_real, back_imag = adjoint_product(link_real, link_imag, real, imag)
    edge_rows = jnp.stack(
        [real[..., :LX], imag[..., :LX], back_real[..., sites - LX :], back_imag[..., sites - LX :]]
    )
    edges = swapped_2(edge_rows, "space", 0)
    next_real = jnp.concatenate([real[..., LX:], edges[0]], axis=3)
    next_imag = jnp.concatenate([imag[..., LX:], edges[1]], axis=3)
    ahead_real, ahead_imag = color_product(link_real, link_imag, next_real, next_imag)
    total_real = (
        total_real + ahead_real + jnp.concatenate([edges[2], back_real[..., : sites - LX]], axis=3)
    )
    total_imag = (
        total_imag + ahead_imag + jnp.concatenate([edges[3], back_imag[..., : sites - LX]], axis=3)
    )
    link_real = link_flat[:, 2, 0]
    link_imag = link_flat[:, 2, 1]
    upper = from_behind(for_sending(jnp.stack([real, imag])), "space", -2)
    ahead_real, ahead_imag = color_product(link_real, link_imag, upper[0], upper[1])
    back_real, back_imag = adjoint_product(link_real, link_imag, real, imag)
    lower = from_behind(for_sending(jnp.stack([back_real, back_imag])), "space", 2)
    total_real = total_real + ahead_real + lower[0]
    total_imag = total_imag + ahead_imag + lower[1]
    return (total_real, total_imag)


def pair_up(field):
    swapped = jnp.stack([field[:, :, 1], -field[:, :, 0]], axis=2)
    return jnp.concatenate([field, swapped], axis=1)


def project(left, right):
    left_flat = left.reshape(left.shape[0], left.shape[1], -1)
    right_flat = right.reshape(right.shape[0], right.shape[1], -1)
    return jnp.einsum("tkm,tvm->tkv", left_flat, right_flat, preferred_element_type=jnp.float32)


def by_planes(solutions, links, eigvecs):
    slices = solutions.shape[0]
    vectors = solutions.shape[1]
    real = solutions[:, :, 0].reshape(slices, vectors, 3, -1)
    imag = solutions[:, :, 1].reshape(slices, vectors, 3, -1)
    link_flat = links.reshape(links.shape[:5] + (-1,))
    for step in range(NSMEAR):
        hop_real, hop_imag = hopping(real, imag, link_flat)
        real = real + kappa_hop * (hop_real - 6.0 * real)
        imag = imag + kappa_hop * (hop_imag - 6.0 * imag)
    smeared = jnp.stack([real, imag], axis=2).reshape(solutions.shape).astype(jnp.bfloat16)
    coefficients = project(eigvecs, pair_up(lax.all_gather(smeared, "space", axis=4, tiled=True)))
    return (smeared, coefficients)


PLANES = 4
FIELDS = 24
LINKS = 54
PARTS = FIELDS + LINKS
WINDOW = PARTS * 8


def is_diagonal(part):
    return part % 18 in (0, 4, 8)


def pack_kernel(place, field, link, edges, *rest):
    outs, wide, windows, narrow = rest[:PLANES], rest[PLANES], rest[PLANES + 1], rest[PLANES + 2]
    z = place[0]
    h = place[1]
    wide[:FIELDS, 2:18, :] = field[...]
    for part in range(LINKS):
        entry = link[part]
        wide[FIELDS + part, 2:18, :] = entry - 1.0 if is_diagonal(part) else entry
    narrow[...] = edges[...].astype(jnp.float32)
    for part in range(PARTS):
        wide[part, 18:20, :] = narrow[4 * part : 4 * part + 2, :]
        wide[part, 0:2, :] = narrow[4 * part + 2 : 4 * part + 4, :]
    for slab in range(PLANES):
        window = wide[:, 4 * slab : 4 * slab + 8, :]
        windows[slab] = window.reshape(WINDOW, 128).astype(jnp.bfloat16)
    for hop in range(PLANES):
        target = lax.rem(z + hop, PLANES)
        slab = jnp.where(h == 0, target, PLANES - 1 - target)
        outs[hop][...] = windows[slab]


def apply_links(matrix, field):
    out = []
    for row in range(3):
        real = imag = None
        for inner in range(3):
            re, im = matrix(row, inner)
            term_real = re * field[inner] - im * field[3 + inner]
            term_imag = re * field[3 + inner] + im * field[inner]
            real = term_real if real is None else real + term_real
            imag = term_imag if imag is None else imag + term_imag
        out.append((real, imag))
    return [pair[0] for pair in out] + [pair[1] for pair in out]


def smear_kernel(place, *rest):
    blocks, out = rest[:PLANES], rest[PLANES]
    phi, links, flat = rest[PLANES + 1 :]
    lane = lax.broadcasted_iota(jnp.int32, (8, 128), 1)
    x_place = lane % LX
    at_end = x_place == LX - 1
    at_start = x_place == 0
    low = lane < LX

    for plane in range(PLANES):
        values = blocks[plane][...].astype(jnp.float32).reshape(PARTS, 8, 128)
        phi[0, plane] = values[:FIELDS]
        for part in range(LINKS):
            entry = values[FIELDS + part]
            links[plane, part] = kappa_hop * (entry + 1.0 if is_diagonal(part) else entry)

    def next_x(a):
        return jnp.where(at_end, pltpu.roll(a, LX - 1, 1), pltpu.roll(a, 127, 1))

    def last_x(a):
        return jnp.where(at_start, pltpu.roll(a, LX + 1, 1), pltpu.roll(a, 1, 1))

    def next_y(a):
        other = pltpu.roll(a, LX, 1)
        return jnp.where(low, other, pltpu.roll(other, 7, 0))

    def last_y(a):
        other = pltpu.roll(a, LX, 1)
        return jnp.where(low, pltpu.roll(other, 1, 0), other)

    def forward(plane, along):
        def entry(row, inner):
            at = along * 18 + row * 3 + inner
            return links[plane, at], links[plane, at + 9]

        return entry

    def backward(plane, along):
        def entry(row, inner):
            at = along * 18 + inner * 3 + row
            return links[plane, at], -links[plane, at + 9]

        return entry

    def one_step(source, target):
        def one(index, carry):
            plane = index // 2
            pair = index % 2
            above = lax.rem(plane + 3, PLANES)
            below = lax.rem(plane + 1, PLANES)
            for vector in range(2):
                base = (pair * 2 + vector) * 6
                field = [phi[source, plane, base + i] for i in range(6)]
                upper = [phi[source, above, base + i] for i in range(6)]
                lower = [phi[source, below, base + i] for i in range(6)]
                total = [(1.0 - 6.0 * kappa_hop) * a for a in field]

                def add(terms):
                    for i in range(6):
                        total[i] = total[i] + terms[i]

                add(apply_links(forward(plane, 0), [next_x(a) for a in field]))
                add([last_x(a) for a in apply_links(backward(plane, 0), field)])
                add(apply_links(forward(plane, 1), [next_y(a) for a in field]))
                add([last_y(a) for a in apply_links(backward(plane, 1), field)])
                add(apply_links(forward(plane, 2), upper))
                add(apply_links(backward(below, 2), lower))
                for i in range(6):
                    phi[target, plane, base + i] = total[i]
            return carry

        lax.fori_loop(0, 2 * PLANES, one, 0)

    for step in range(NSMEAR):
        one_step(step % 2, (step + 1) % 2)

    last = NSMEAR % 2
    for plane in range(PLANES):
        true_plane = lax.rem(place[0] + PLANES - plane, PLANES)
        for row in range(4):
            flat[true_plane, :, row * 128 : (row + 1) * 128] = phi[last, plane, :, 2 + row, :]
    out[...] = flat[...].reshape(PLANES * FIELDS, 512).astype(jnp.bfloat16)


def project_kernel(place, eigvecs, masks, *rest):
    own, other = rest[:PLANES], rest[PLANES : 2 * PLANES]
    smeared, coefficients, sites, column = rest[2 * PLANES :]
    z = place[0]
    h = place[1]
    half = PLANES * FIELDS
    for hop in range(PLANES):
        origin = lax.rem(z + PLANES - hop, PLANES)
        for blocks, side in ((own, h), (other, 1 - h)):
            slab = jnp.where(side == 0, origin, PLANES - 1 - origin)
            rows = pl.ds(pl.multiple_of(side * half, half), half)
            columns = pl.ds(pl.multiple_of(slab * 512, 512), 512)
            sites[rows, columns] = blocks[hop][...]
            if blocks is own:
                wide = blocks[hop][...].astype(jnp.float32)
                column[:, :, columns] = wide.reshape(PLANES, FIELDS, 512)
    smeared[...] = column[z].astype(jnp.bfloat16)
    vector = masks[96:97, :]
    count = 4
    for group in range(eigvecs.shape[0] // (48 * count)):
        rows = eigvecs[group * 48 * count : (group + 1) * 48 * count, :]
        product = lax.dot_general(
            rows, sites[...], (((1,), (1,)), ((), ())), preferred_element_type=jnp.float32
        ).reshape(count, 48, 2 * half)
        for at, mask in ((0, masks[0:48, :]), (4, masks[48:96, :])):
            sums = jnp.sum(product * mask[None], axis=1)
            for v in range(4):
                picked = jnp.where(vector == float(v), sums, 0.0)
                coefficients[group * count : (group + 1) * count, at + v : at + v + 1] = jnp.sum(
                    picked, axis=1, keepdims=True
                )


def projection_masks():
    row = np.arange(48)[:, None]
    ri, color, r = row // 24, row // 8 % 3, row % 8
    column = np.arange(192)[None]
    h, z, v = column // 96, column // 24 % 4, column // 6 % 4
    ri_right, color_right = column // 3 % 2, column % 3
    here = (color == color_right) & (r == 2 * z + h)
    real = np.where(here & (ri == ri_right), 1.0, 0.0)
    imag = np.where(here & (ri != ri_right), np.where(ri == 0, 1.0, -1.0), 0.0)
    vectors = np.broadcast_to(v, (8, 192))
    return np.concatenate([real, imag, vectors]).astype(np.float32)


def on_device(count):
    return [pl.BlockSpec(memory_space=pltpu.VMEM)] * count


def in_slabs(solutions, links, eigvecs):
    me = lax.axis_index("space")
    place = jnp.stack([me // 2, me % 2]).astype(jnp.int32)
    scalars = [pl.BlockSpec(memory_space=pltpu.SMEM)]
    limit = pltpu.CompilerParams(vmem_limit_bytes=32 * 1024 * 1024)

    def swapped(block):
        return lax.ppermute(block, "space", [(i, i ^ 1) for i in range(2 * PLANES)])

    def moved_up(block, planes):
        count = 2 * PLANES
        return lax.ppermute(block, "space", [(i, (i + 2 * planes) % count) for i in range(count)])

    field = solutions.reshape(FIELDS, 16, 128)
    link = links.reshape(LINKS, 16, 128)
    unit = np.array([1.0 if is_diagonal(part) else 0.0 for part in range(LINKS)], np.float32)
    both = jnp.concatenate([field, link - unit[:, None, None]])
    edges = jnp.concatenate([both[:, 0:2], both[:, 14:16]], axis=1).astype(jnp.bfloat16)
    edges = swapped(edges.reshape(4 * PARTS, 128))
    window = jax.ShapeDtypeStruct((WINDOW, 128), jnp.bfloat16)
    windows = pl.pallas_call(
        pack_kernel,
        out_shape=[window] * PLANES,
        in_specs=scalars + on_device(3),
        out_specs=on_device(PLANES),
        scratch_shapes=[
            pltpu.VMEM((PARTS, 24, 128), jnp.float32),
            pltpu.VMEM((PLANES, WINDOW, 128), jnp.bfloat16),
            pltpu.VMEM((4 * PARTS, 128), jnp.float32),
        ],
        compiler_params=limit,
        name="pack",
    )(place, field, link, edges)
    blocks = [windows[0]] + [moved_up(windows[hop], hop) for hop in range(1, PLANES)]
    block = pl.pallas_call(
        smear_kernel,
        out_shape=jax.ShapeDtypeStruct((PLANES * FIELDS, 512), jnp.bfloat16),
        in_specs=scalars + on_device(PLANES),
        out_specs=pl.BlockSpec(memory_space=pltpu.VMEM),
        scratch_shapes=[
            pltpu.VMEM((2, PLANES, FIELDS, 8, 128), jnp.float32),
            pltpu.VMEM((PLANES, LINKS, 8, 128), jnp.float32),
            pltpu.VMEM((PLANES, FIELDS, 512), jnp.float32),
        ],
        compiler_params=limit,
        name="smear",
    )(place, *blocks)
    own = [block] + [moved_up(block, hop) for hop in range(1, PLANES)]
    other = [swapped(part) for part in own]
    vectors = eigvecs.shape[1]
    smeared, coefficients = pl.pallas_call(
        project_kernel,
        out_shape=[
            jax.ShapeDtypeStruct((FIELDS, 2048), jnp.bfloat16),
            jax.ShapeDtypeStruct((vectors, 8), jnp.float32),
        ],
        in_specs=scalars + on_device(2 + 2 * PLANES),
        out_specs=on_device(2),
        scratch_shapes=[
            pltpu.VMEM((2 * PLANES * FIELDS, 2048), jnp.bfloat16),
            pltpu.VMEM((PLANES, FIELDS, 2048), jnp.float32),
        ],
        compiler_params=limit,
        name="project",
    )(place, eigvecs.reshape(vectors * 48, 2048), projection_masks(), *own, *other)
    return smeared.reshape(solutions.shape), coefficients[None]


def local(solutions, links, eigvecs):
    fits = lax.axis_size("space") == 2 * PLANES and solutions.shape[:2] == (1, 4)
    fits = fits and solutions.shape[4:] == (1, 2048) and eigvecs.shape[1] % 4 == 0
    return (in_slabs if fits else by_planes)(solutions, links, eigvecs)


def solution(mesh):
    placed = (
        P(("cfg", "tm"), None, None, None, "space", None),
        P(("cfg", "tm"), None, None, None, None, "space", None),
        P(("cfg", "tm"), "space", None, None, None, None),
    )
    return jax.shard_map(
        local,
        mesh=mesh,
        in_specs=placed,
        out_specs=(
            P(("cfg", "tm"), None, None, None, "space", None),
            P(("cfg", "tm"), "space", None),
        ),
        check_vma=False,
    )
```

```python
import jax
import jax.numpy as jnp
from jax import lax
from jax.experimental import pallas as pl
from jax.experimental.pallas import tpu as pltpu
from jax.sharding import PartitionSpec as P

NSMEAR = 4
LX = 64


kappa_hop = 0.1


def swapped_2(block, axis, stride):
    count = lax.axis_size(axis)
    route = []
    for low in range(count):
        high = low | 1 << stride
        if high != low and high < count:
            route += [(low, high), (high, low)]
    return lax.ppermute(block, axis, route)


def for_sending(array):

    def short(part):
        return part.astype(jnp.bfloat16) if part.dtype == jnp.float32 else part

    return jax.tree.map(short, array)


def from_behind(block, axis, distance):
    devices = range(lax.axis_size(axis))
    route = [((i - distance) % len(devices), i) for i in devices]
    return lax.ppermute(block, axis, route)


def color_product(link_real, link_imag, field_real, field_imag):
    out_real = None
    out_imag = None
    for inner in range(3):
        column_real = link_real[:, None, :, inner]
        column_imag = link_imag[:, None, :, inner]
        entry_real = field_real[:, :, inner : inner + 1]
        entry_imag = field_imag[:, :, inner : inner + 1]
        term_real = column_real * entry_real - column_imag * entry_imag
        term_imag = column_real * entry_imag + column_imag * entry_real
        if out_real is None:
            out_real = term_real
            out_imag = term_imag
        else:
            out_real = out_real + term_real
            out_imag = out_imag + term_imag
    return (out_real, out_imag)


def adjoint_product(link_real, link_imag, field_real, field_imag):
    return color_product(
        jnp.swapaxes(link_real, 1, 2), -jnp.swapaxes(link_imag, 1, 2), field_real, field_imag
    )


def hopping(real, imag, link_flat):
    sites = real.shape[-1]
    x_place = lax.broadcasted_iota(jnp.int32, (sites,), 0) % LX
    at_end = x_place == LX - 1
    at_start = x_place == 0
    link_real = link_flat[:, 0, 0]
    link_imag = link_flat[:, 0, 1]
    next_real = jnp.where(at_end, jnp.roll(real, LX - 1, 3), jnp.roll(real, -1, 3))
    next_imag = jnp.where(at_end, jnp.roll(imag, LX - 1, 3), jnp.roll(imag, -1, 3))
    ahead_real, ahead_imag = color_product(link_real, link_imag, next_real, next_imag)
    back_real, back_imag = adjoint_product(link_real, link_imag, real, imag)
    total_real = ahead_real + jnp.where(
        at_start, jnp.roll(back_real, 1 - LX, 3), jnp.roll(back_real, 1, 3)
    )
    total_imag = ahead_imag + jnp.where(
        at_start, jnp.roll(back_imag, 1 - LX, 3), jnp.roll(back_imag, 1, 3)
    )
    link_real = link_flat[:, 1, 0]
    link_imag = link_flat[:, 1, 1]
    back_real, back_imag = adjoint_product(link_real, link_imag, real, imag)
    edge_rows = jnp.stack(
        [real[..., :LX], imag[..., :LX], back_real[..., sites - LX :], back_imag[..., sites - LX :]]
    )
    edges = swapped_2(edge_rows, "space", 0)
    next_real = jnp.concatenate([real[..., LX:], edges[0]], axis=3)
    next_imag = jnp.concatenate([imag[..., LX:], edges[1]], axis=3)
    ahead_real, ahead_imag = color_product(link_real, link_imag, next_real, next_imag)
    total_real = (
        total_real + ahead_real + jnp.concatenate([edges[2], back_real[..., : sites - LX]], axis=3)
    )
    total_imag = (
        total_imag + ahead_imag + jnp.concatenate([edges[3], back_imag[..., : sites - LX]], axis=3)
    )
    link_real = link_flat[:, 2, 0]
    link_imag = link_flat[:, 2, 1]
    upper = from_behind(for_sending(jnp.stack([real, imag])), "space", -2)
    ahead_real, ahead_imag = color_product(link_real, link_imag, upper[0], upper[1])
    back_real, back_imag = adjoint_product(link_real, link_imag, real, imag)
    lower = from_behind(for_sending(jnp.stack([back_real, back_imag])), "space", 2)
    total_real = total_real + ahead_real + lower[0]
    total_imag = total_imag + ahead_imag + lower[1]
    return (total_real, total_imag)


def pair_up(field):
    swapped = jnp.stack([field[:, :, 1], -field[:, :, 0]], axis=2)
    return jnp.concatenate([field, swapped], axis=1)


def project(left, right):
    left_flat = left.reshape(left.shape[0], left.shape[1], -1)
    right_flat = right.reshape(right.shape[0], right.shape[1], -1)
    return jnp.einsum("tkm,tvm->tkv", left_flat, right_flat, preferred_element_type=jnp.float32)


def by_planes(solutions, links, eigvecs):
    slices = solutions.shape[0]
    vectors = solutions.shape[1]
    real = solutions[:, :, 0].reshape(slices, vectors, 3, -1)
    imag = solutions[:, :, 1].reshape(slices, vectors, 3, -1)
    link_flat = links.reshape(links.shape[:5] + (-1,))
    for step in range(NSMEAR):
        hop_real, hop_imag = hopping(real, imag, link_flat)
        real = real + kappa_hop * (hop_real - 6.0 * real)
        imag = imag + kappa_hop * (hop_imag - 6.0 * imag)
    smeared = jnp.stack([real, imag], axis=2).reshape(solutions.shape).astype(jnp.bfloat16)
    coefficients = project(eigvecs, pair_up(lax.all_gather(smeared, "space", axis=4, tiled=True)))
    return (smeared, coefficients)


PLANES = 4
FIELDS = 24
LINKS = 54
PARTS = FIELDS + LINKS
WINDOW = PARTS * 8


def is_diagonal(part):
    return part >= FIELDS and (part - FIELDS) % 18 in (0, 4, 8)


def my_place():
    me = lax.axis_index("space")
    return me // 2, lax.rem(me, 2)


def slab_of(z, h):
    return jnp.where(h == 0, z, PLANES - 1 - z)


def read_kernel(field, link, ends, wide, narrow, field_done, link_done):
    field_copy = pltpu.make_async_copy(field, wide.at[:FIELDS], field_done)
    link_copy = pltpu.make_async_copy(link, wide.at[FIELDS:], link_done)
    field_copy.start()
    link_copy.start()
    field_copy.wait()
    link_copy.wait()
    for part in range(PARTS):
        if is_diagonal(part):
            wide[part] = wide[part] - 1.0
        narrow[4 * part : 4 * part + 2, :] = wide[part, 0:2, :]
        narrow[4 * part + 2 : 4 * part + 4, :] = wide[part, 14:16, :]
    ends[...] = narrow[...].astype(jnp.bfloat16)


def pack_kernel(wide, ends, *rest):
    outs, window, windows, narrow = rest[:PLANES], *rest[PLANES:]
    z, h = my_place()
    narrow[...] = ends[...].astype(jnp.float32)
    for slab in range(PLANES):
        low, high = max(4 * slab - 2, 0), min(4 * slab + 6, 16)
        to = low - (4 * slab - 2)
        window[:, to : to + high - low, :] = wide[:, low:high, :]
        for part in range(PARTS):
            if slab == 0:
                window[part, 0:2, :] = narrow[4 * part + 2 : 4 * part + 4, :]
            if slab == PLANES - 1:
                window[part, 6:8, :] = narrow[4 * part : 4 * part + 2, :]
        windows[slab] = window[...].reshape(WINDOW, 128).astype(jnp.bfloat16)
    for hop in range(PLANES):
        outs[hop][...] = windows[slab_of(lax.rem(z + hop, PLANES), h)]


def by_color(part):
    vector, rest = part // 6, part % 6
    return vector * 6 + rest % 3 * 2 + rest // 3


def apply_links(entry, sign, field):
    reals = []
    imags = []
    for row in range(3):
        real = imag = None
        for inner in range(3):
            re, im = entry(row, inner)
            real_a, real_b = re * field[inner], im * field[3 + inner]
            imag_a, imag_b = re * field[3 + inner], im * field[inner]
            if sign > 0:
                term_real, term_imag = real_a - real_b, imag_a + imag_b
            else:
                term_real, term_imag = real_a + real_b, imag_a - imag_b
            real = term_real if real is None else real + term_real
            imag = term_imag if imag is None else imag + term_imag
        reals.append(real)
        imags.append(imag)
    return reals + imags


def smear_kernel(*rest):
    blocks, (out, phi, links, flat) = rest[:PLANES], rest[PLANES:]
    lane = lax.broadcasted_iota(jnp.int32, (8, 128), 1)
    x_place = lane % LX
    at_end = x_place == LX - 1
    at_start = x_place == 0
    low = lane < LX

    def scaled(part, value):
        return kappa_hop * (value + 1.0 if is_diagonal(part) else value)

    for plane in range(PLANES):
        values = blocks[plane][...].astype(jnp.float32).reshape(PARTS, 8, 128)
        for part in range(FIELDS):
            phi[0, plane, by_color(part)] = values[part]
        for part in range(FIELDS, PARTS):
            links[plane, part - FIELDS] = scaled(part, values[part])

    def next_x(a):
        return jnp.where(at_end, pltpu.roll(a, LX - 1, 1), pltpu.roll(a, 127, 1))

    def last_x(a):
        return jnp.where(at_start, pltpu.roll(a, LX + 1, 1), pltpu.roll(a, 1, 1))

    def next_y(a):
        other = pltpu.roll(a, LX, 1)
        return jnp.where(low, other, pltpu.roll(other, 7, 0))

    def last_y(a):
        other = pltpu.roll(a, LX, 1)
        return jnp.where(low, pltpu.roll(other, 1, 0), other)

    def forward(plane, along, field):
        def entry(row, inner):
            at = along * 18 + row * 3 + inner
            return links[plane, at], links[plane, at + 9]

        return apply_links(entry, 1, field)

    def backward(plane, along, field):
        def entry(row, inner):
            at = along * 18 + inner * 3 + row
            return links[plane, at], links[plane, at + 9]

        return apply_links(entry, -1, field)

    def one_step(source, target):
        def one(plane, carry):
            above = lax.rem(plane + 3, PLANES)
            below = lax.rem(plane + 1, PLANES)
            for vector in range(FIELDS // 6):
                base = vector * 6
                field = [phi[source, plane, base + by_color(i)] for i in range(6)]
                upper = [phi[source, above, base + by_color(i)] for i in range(6)]
                lower = [phi[source, below, base + by_color(i)] for i in range(6)]
                total = [(1.0 - 6.0 * kappa_hop) * a for a in field]
                for terms in (
                    [last_x(a) for a in backward(plane, 0, field)],
                    [last_y(a) for a in backward(plane, 1, field)],
                    forward(plane, 2, upper),
                    backward(below, 2, lower),
                    forward(plane, 0, [next_x(a) for a in field]),
                    forward(plane, 1, [next_y(a) for a in field]),
                ):
                    total = [a + b for a, b in zip(total, terms)]
                for i in range(6):
                    phi[target, plane, base + by_color(i)] = total[i]
            return carry

        lax.fori_loop(0, PLANES, one, 0)

    for step in range(NSMEAR):
        one_step(step % 2, (step + 1) % 2)

    last = NSMEAR % 2
    for plane in range(PLANES):
        true_plane = lax.rem(my_place()[0] + PLANES - plane, PLANES)
        for row in range(4):
            flat[true_plane, :, row * 128 : (row + 1) * 128] = phi[last, plane, :, 2 + row, :]
    out[...] = flat[...].reshape(PLANES * FIELDS, 512).astype(jnp.bfloat16)


def column_start(z, hop, side):
    slab = slab_of(lax.rem(z + PLANES - hop, PLANES), side)
    return pl.ds(pl.multiple_of(slab * 512, 512), 512)


def own_plane_kernel(*rest):
    blocks, out, column = rest[:PLANES], rest[PLANES], rest[PLANES + 1]
    z, h = my_place()
    for hop in range(PLANES):
        block = blocks[hop][...].astype(jnp.float32).reshape(PLANES, FIELDS, 512)
        column[:, :, column_start(z, hop, h)] = block
    out[...] = column[z].reshape(out.shape).astype(jnp.bfloat16)


FAR = 2


def reduce_sites(eigvecs, columns, sites, masks, vectors, sums):
    count = 4
    width = sites.shape[0]
    for group in range(eigvecs.shape[0] // (48 * count)):
        rows = eigvecs[group * 48 * count : (group + 1) * 48 * count, columns]
        product = lax.dot_general(
            rows, sites[...], (((1,), (1,)), ((), ())), preferred_element_type=jnp.float32
        ).reshape(count, 48, width)
        for part in range(2):
            sums[part, group * count : (group + 1) * count, :] = jnp.sum(
                product * masks[part][None], axis=1
            )
    return [
        lax.dot_general(
            vectors,
            sums[part],
            (((1,), (1,)), ((), ())),
            precision=lax.Precision.HIGHEST,
            preferred_element_type=jnp.float32,
        )[:4]
        for part in range(2)
    ]


def project_near_kernel(eigvecs, *rest):
    own, other = rest[:PLANES], list(rest[PLANES : 2 * PLANES - 1])
    coefficients, sites, sums = rest[2 * PLANES - 1 :]
    other.insert(FAR, None)
    half = PLANES * FIELDS
    z, h = my_place()
    for hop in range(PLANES):
        for blocks, side in ((own, h), (other, 1 - h)):
            rows = pl.ds(pl.multiple_of(side * half, half), half)
            here = jnp.zeros((half, 512), jnp.bfloat16) if blocks[hop] is None else blocks[hop][...]
            sites[rows, column_start(z, hop, side)] = here
    masks, vectors = projection_masks(2 * half, 0)
    parts = reduce_sites(eigvecs, slice(None), sites, masks, vectors, sums)
    for part in range(2):
        coefficients[4 * part : 4 * part + 4, :] = parts[part]


def project_far_kernel(eigvecs, near, block, coefficients, sums):
    z, h = my_place()
    masks, vectors = projection_masks(PLANES * FIELDS, 1 - h)
    parts = reduce_sites(eigvecs, column_start(z, FAR, 1 - h), block, masks, vectors, sums)
    for part in range(2):
        rows = slice(4 * part, 4 * part + 4)
        coefficients[rows, :] = near[rows, :] + parts[part]


def divided(a, by):
    return lax.shift_right_logical(a * (65536 // by + 1), 16)


def projection_masks(width, side):
    shape = (48, width)
    row = lax.broadcasted_iota(jnp.int32, shape, 0)
    column = lax.broadcasted_iota(jnp.int32, shape, 1)
    ri = lax.shift_right_logical(row + 8, 5)
    color = lax.shift_right_logical(row, 3) - 3 * ri
    pair = lax.shift_right_logical(column, 1)
    ri_right = column - 2 * pair
    vector = divided(pair, 3)
    color_right = pair - 3 * vector
    site_row = divided(column, FIELDS)
    site_row = 2 * (site_row & 3) + lax.shift_right_logical(site_row, 2) + side
    here = (color == color_right) & ((row & 7) == site_row)
    real = jnp.where(here & (ri == ri_right), 1.0, 0.0)
    imag = jnp.where(here & (ri != ri_right), jnp.where(ri == 0, 1.0, -1.0), 0.0)
    vectors = jnp.where((vector & 3)[:8] == lax.broadcasted_iota(jnp.int32, (8, shape[1]), 0), 1.0, 0.0)
    return (real, imag), vectors


def in_vmem(count):
    return [pl.BlockSpec(memory_space=pltpu.VMEM)] * count


def in_slabs(solutions, links, eigvecs):
    in_hbm = [pl.BlockSpec(memory_space=pltpu.HBM)]
    limit = pltpu.CompilerParams(vmem_limit_bytes=8 * 1024 * 1024)
    count = 2 * PLANES

    def swapped(block):
        return lax.ppermute(block, "space", [(i, i ^ 1) for i in range(count)])

    def moved_up(block, planes):
        return lax.ppermute(block, "space", [(i, (i + 2 * planes) % count) for i in range(count)])

    ends, wide = pl.pallas_call(
        read_kernel,
        out_shape=[
            jax.ShapeDtypeStruct((4 * PARTS, 128), jnp.bfloat16),
            jax.ShapeDtypeStruct((PARTS, 16, 128), jnp.float32),
        ],
        in_specs=in_hbm * 2,
        out_specs=in_vmem(2),
        scratch_shapes=[
            pltpu.VMEM((4 * PARTS, 128), jnp.float32),
            pltpu.SemaphoreType.DMA(()),
            pltpu.SemaphoreType.DMA(()),
        ],
        compiler_params=pltpu.CompilerParams(vmem_limit_bytes=63 * 1024 * 1024),
        name="read",
    )(solutions.reshape(FIELDS, 16, 128), links.reshape(LINKS, 16, 128))
    packed = pl.pallas_call(
        pack_kernel,
        out_shape=[jax.ShapeDtypeStruct((WINDOW, 128), jnp.bfloat16)] * PLANES,
        in_specs=in_vmem(2),
        out_specs=in_vmem(PLANES),
        scratch_shapes=[
            pltpu.VMEM((PARTS, 8, 128), jnp.float32),
            pltpu.VMEM((PLANES, WINDOW, 128), jnp.bfloat16),
            pltpu.VMEM((4 * PARTS, 128), jnp.float32),
        ],
        compiler_params=limit,
        name="pack",
    )(wide, swapped(ends))
    vectors = eigvecs.shape[1]
    blocks = [packed[0]] + [moved_up(packed[hop], hop) for hop in range(1, PLANES)]
    vectors = eigvecs.shape[1]
    block = pl.pallas_call(
        smear_kernel,
        out_shape=jax.ShapeDtypeStruct((PLANES * FIELDS, 512), jnp.bfloat16),
        in_specs=in_vmem(PLANES),
        out_specs=pl.BlockSpec(memory_space=pltpu.VMEM),
        scratch_shapes=[
            pltpu.VMEM((2, PLANES, FIELDS, 8, 128), jnp.float32),
            pltpu.VMEM((PLANES, LINKS, 8, 128), jnp.float32),
            pltpu.VMEM((PLANES, FIELDS, 512), jnp.float32),
        ],
        compiler_params=limit,
        cost_estimate=pl.CostEstimate(flops=10**9, bytes_accessed=2 * 10**7, transcendentals=0),
        name="smear",
    )(*blocks)
    own = [block] + [moved_up(block, hop) for hop in range(1, PLANES)]
    own[FAR] = lax.optimization_barrier((own[FAR], own[1], own[3]))[0]
    other = [swapped(part) for part in own]
    smeared = pl.pallas_call(
        own_plane_kernel,
        out_shape=jax.ShapeDtypeStruct((FIELDS // 2, 2, 2048), jnp.bfloat16),
        in_specs=in_vmem(PLANES),
        out_specs=pl.BlockSpec(memory_space=pltpu.VMEM),
        scratch_shapes=[pltpu.VMEM((PLANES, FIELDS, 2048), jnp.float32)],
        compiler_params=limit,
        name="own_plane",
    )(*own)
    eigvecs = eigvecs.reshape(vectors * 48, 2048)
    near = pl.pallas_call(
        project_near_kernel,
        out_shape=jax.ShapeDtypeStruct((8, vectors), jnp.float32),
        in_specs=in_vmem(2 * PLANES),
        out_specs=pl.BlockSpec(memory_space=pltpu.VMEM),
        scratch_shapes=[
            pltpu.VMEM((2 * PLANES * FIELDS, 2048), jnp.bfloat16),
            pltpu.VMEM((2, vectors, 2 * PLANES * FIELDS), jnp.float32),
        ],
        compiler_params=limit,
        cost_estimate=pl.CostEstimate(flops=10**9, bytes_accessed=4 * 10**6, transcendentals=0),
        name="project_near",
    )(eigvecs, *own, *other[:FAR], *other[FAR + 1 :])
    coefficients = pl.pallas_call(
        project_far_kernel,
        out_shape=jax.ShapeDtypeStruct((8, vectors), jnp.float32),
        in_specs=in_vmem(3),
        out_specs=pl.BlockSpec(memory_space=pltpu.VMEM),
        scratch_shapes=[pltpu.VMEM((2, vectors, PLANES * FIELDS), jnp.float32)],
        compiler_params=limit,
        name="project_far",
    )(eigvecs, near, other[FAR])
    smeared = smeared.reshape(1, 4, 3, 2, 1, 2048).swapaxes(2, 3)
    return smeared, coefficients.T[None]


def local(solutions, links, eigvecs):
    fits = lax.axis_size("space") == 2 * PLANES and solutions.shape[:2] == (1, 4)
    fits = fits and solutions.shape[4:] == (1, 2048) and eigvecs.shape[1] % 4 == 0
    return (in_slabs if fits else by_planes)(solutions, links, eigvecs)


def solution(mesh):
    placed = (
        P(("cfg", "tm"), None, None, None, "space", None),
        P(("cfg", "tm"), None, None, None, None, "space", None),
        P(("cfg", "tm"), "space", None, None, None, None),
    )
    return jax.shard_map(
        local,
        mesh=mesh,
        in_specs=placed,
        out_specs=(
            P(("cfg", "tm"), None, None, None, "space", None),
            P(("cfg", "tm"), "space", None),
        ),
        check_vma=False,
    )
```

```python
import jax
import jax.numpy as jnp
from jax import lax
from jax.experimental import pallas as pl
from jax.experimental.pallas import tpu as pltpu
from jax.sharding import PartitionSpec as P

NSMEAR = 4
LX = 64


kappa_hop = 0.1


def swapped_2(block, axis, stride):
    count = lax.axis_size(axis)
    route = []
    for low in range(count):
        high = low | 1 << stride
        if high != low and high < count:
            route += [(low, high), (high, low)]
    return lax.ppermute(block, axis, route)


def for_sending(array):

    def short(part):
        return part.astype(jnp.bfloat16) if part.dtype == jnp.float32 else part

    return jax.tree.map(short, array)


def from_behind(block, axis, distance):
    devices = range(lax.axis_size(axis))
    route = [((i - distance) % len(devices), i) for i in devices]
    return lax.ppermute(block, axis, route)


def color_product(link_real, link_imag, field_real, field_imag):
    out_real = None
    out_imag = None
    for inner in range(3):
        column_real = link_real[:, None, :, inner]
        column_imag = link_imag[:, None, :, inner]
        entry_real = field_real[:, :, inner : inner + 1]
        entry_imag = field_imag[:, :, inner : inner + 1]
        term_real = column_real * entry_real - column_imag * entry_imag
        term_imag = column_real * entry_imag + column_imag * entry_real
        if out_real is None:
            out_real = term_real
            out_imag = term_imag
        else:
            out_real = out_real + term_real
            out_imag = out_imag + term_imag
    return (out_real, out_imag)


def adjoint_product(link_real, link_imag, field_real, field_imag):
    return color_product(
        jnp.swapaxes(link_real, 1, 2), -jnp.swapaxes(link_imag, 1, 2), field_real, field_imag
    )


def hopping(real, imag, link_flat):
    sites = real.shape[-1]
    x_place = lax.broadcasted_iota(jnp.int32, (sites,), 0) % LX
    at_end = x_place == LX - 1
    at_start = x_place == 0
    link_real = link_flat[:, 0, 0]
    link_imag = link_flat[:, 0, 1]
    next_real = jnp.where(at_end, jnp.roll(real, LX - 1, 3), jnp.roll(real, -1, 3))
    next_imag = jnp.where(at_end, jnp.roll(imag, LX - 1, 3), jnp.roll(imag, -1, 3))
    ahead_real, ahead_imag = color_product(link_real, link_imag, next_real, next_imag)
    back_real, back_imag = adjoint_product(link_real, link_imag, real, imag)
    total_real = ahead_real + jnp.where(
        at_start, jnp.roll(back_real, 1 - LX, 3), jnp.roll(back_real, 1, 3)
    )
    total_imag = ahead_imag + jnp.where(
        at_start, jnp.roll(back_imag, 1 - LX, 3), jnp.roll(back_imag, 1, 3)
    )
    link_real = link_flat[:, 1, 0]
    link_imag = link_flat[:, 1, 1]
    back_real, back_imag = adjoint_product(link_real, link_imag, real, imag)
    edge_rows = jnp.stack(
        [real[..., :LX], imag[..., :LX], back_real[..., sites - LX :], back_imag[..., sites - LX :]]
    )
    edges = swapped_2(edge_rows, "space", 0)
    next_real = jnp.concatenate([real[..., LX:], edges[0]], axis=3)
    next_imag = jnp.concatenate([imag[..., LX:], edges[1]], axis=3)
    ahead_real, ahead_imag = color_product(link_real, link_imag, next_real, next_imag)
    total_real = (
        total_real + ahead_real + jnp.concatenate([edges[2], back_real[..., : sites - LX]], axis=3)
    )
    total_imag = (
        total_imag + ahead_imag + jnp.concatenate([edges[3], back_imag[..., : sites - LX]], axis=3)
    )
    link_real = link_flat[:, 2, 0]
    link_imag = link_flat[:, 2, 1]
    upper = from_behind(for_sending(jnp.stack([real, imag])), "space", -2)
    ahead_real, ahead_imag = color_product(link_real, link_imag, upper[0], upper[1])
    back_real, back_imag = adjoint_product(link_real, link_imag, real, imag)
    lower = from_behind(for_sending(jnp.stack([back_real, back_imag])), "space", 2)
    total_real = total_real + ahead_real + lower[0]
    total_imag = total_imag + ahead_imag + lower[1]
    return (total_real, total_imag)


def pair_up(field):
    swapped = jnp.stack([field[:, :, 1], -field[:, :, 0]], axis=2)
    return jnp.concatenate([field, swapped], axis=1)


def project(left, right):
    left_flat = left.reshape(left.shape[0], left.shape[1], -1)
    right_flat = right.reshape(right.shape[0], right.shape[1], -1)
    return jnp.einsum("tkm,tvm->tkv", left_flat, right_flat, preferred_element_type=jnp.float32)


def by_planes(solutions, links, eigvecs):
    slices = solutions.shape[0]
    vectors = solutions.shape[1]
    real = solutions[:, :, 0].reshape(slices, vectors, 3, -1)
    imag = solutions[:, :, 1].reshape(slices, vectors, 3, -1)
    link_flat = links.reshape(links.shape[:5] + (-1,))
    for step in range(NSMEAR):
        hop_real, hop_imag = hopping(real, imag, link_flat)
        real = real + kappa_hop * (hop_real - 6.0 * real)
        imag = imag + kappa_hop * (hop_imag - 6.0 * imag)
    smeared = jnp.stack([real, imag], axis=2).reshape(solutions.shape).astype(jnp.bfloat16)
    coefficients = project(eigvecs, pair_up(lax.all_gather(smeared, "space", axis=4, tiled=True)))
    return (smeared, coefficients)


PLANES = 4
FIELDS = 24
LINKS = 54
PARTS = FIELDS + LINKS
WINDOW = PARTS * 8


def is_diagonal(part):
    return part >= FIELDS and (part - FIELDS) % 18 in (0, 4, 8)


def my_place():
    me = lax.axis_index("space")
    return me // 2, lax.rem(me, 2)


def slab_of(z, h):
    return jnp.where(h == 0, z, PLANES - 1 - z)


def read_kernel(field, link, ends, wide, narrow, field_done, link_done):
    field_copy = pltpu.make_async_copy(field, wide.at[:FIELDS], field_done)
    link_copy = pltpu.make_async_copy(link, wide.at[FIELDS:], link_done)
    field_copy.start()
    link_copy.start()
    field_copy.wait()
    link_copy.wait()
    for part in range(PARTS):
        if is_diagonal(part):
            wide[part] = wide[part] - 1.0
        narrow[4 * part : 4 * part + 2, :] = wide[part, 0:2, :]
        narrow[4 * part + 2 : 4 * part + 4, :] = wide[part, 14:16, :]
    ends[...] = narrow[...].astype(jnp.bfloat16)


def pack_kernel(wide, ends, *rest):
    outs, window, windows, narrow = rest[:PLANES], *rest[PLANES:]
    z, h = my_place()
    narrow[...] = ends[...].astype(jnp.float32)
    for slab in range(PLANES):
        low, high = max(4 * slab - 2, 0), min(4 * slab + 6, 16)
        to = low - (4 * slab - 2)
        window[:, to : to + high - low, :] = wide[:, low:high, :]
        for part in range(PARTS):
            if slab == 0:
                window[part, 0:2, :] = narrow[4 * part + 2 : 4 * part + 4, :]
            if slab == PLANES - 1:
                window[part, 6:8, :] = narrow[4 * part : 4 * part + 2, :]
        windows[slab] = window[...].reshape(WINDOW, 128).astype(jnp.bfloat16)
    for hop in range(PLANES):
        outs[hop][...] = windows[slab_of(z ^ hop, h)]


def by_color(part):
    vector, rest = part // 6, part % 6
    return vector * 6 + rest % 3 * 2 + rest // 3


def apply_links(entry, sign, field):
    reals = []
    imags = []
    for row in range(3):
        real = imag = None
        for inner in range(3):
            re, im = entry(row, inner)
            real_a, real_b = re * field[inner], im * field[3 + inner]
            imag_a, imag_b = re * field[3 + inner], im * field[inner]
            if sign > 0:
                term_real, term_imag = real_a - real_b, imag_a + imag_b
            else:
                term_real, term_imag = real_a + real_b, imag_a - imag_b
            real = term_real if real is None else real + term_real
            imag = term_imag if imag is None else imag + term_imag
        reals.append(real)
        imags.append(imag)
    return reals + imags


def smear_kernel(*rest):
    blocks, (out, phi, links, flat) = rest[:PLANES], rest[PLANES:]
    lane = lax.broadcasted_iota(jnp.int32, (8, 128), 1)
    x_place = lane % LX
    at_end = x_place == LX - 1
    at_start = x_place == 0
    low = lane < LX

    z, _ = my_place()
    up = 1 + 2 * lax.rem(z, 2)

    def scaled(part, value):
        return kappa_hop * (value + 1.0 if is_diagonal(part) else value)

    for plane in range(PLANES):
        values = blocks[plane][...].astype(jnp.float32).reshape(PARTS, 8, 128)
        for part in range(FIELDS):
            phi[0, plane, by_color(part)] = values[part]
        for part in range(FIELDS, PARTS):
            links[plane, part - FIELDS] = scaled(part, values[part])

    def next_x(a):
        return jnp.where(at_end, pltpu.roll(a, LX - 1, 1), pltpu.roll(a, 127, 1))

    def last_x(a):
        return jnp.where(at_start, pltpu.roll(a, LX + 1, 1), pltpu.roll(a, 1, 1))

    def next_y(a):
        other = pltpu.roll(a, LX, 1)
        return jnp.where(low, other, pltpu.roll(other, 7, 0))

    def last_y(a):
        other = pltpu.roll(a, LX, 1)
        return jnp.where(low, pltpu.roll(other, 1, 0), other)

    def forward(plane, along, field):
        def entry(row, inner):
            at = along * 18 + row * 3 + inner
            return links[plane, at], links[plane, at + 9]

        return apply_links(entry, 1, field)

    def backward(plane, along, field):
        def entry(row, inner):
            at = along * 18 + inner * 3 + row
            return links[plane, at], links[plane, at + 9]

        return apply_links(entry, -1, field)

    def one_step(source, target):
        def one(plane, carry):
            above = lax.rem(plane + up, PLANES)
            below = lax.rem(plane + PLANES - up, PLANES)
            for vector in range(FIELDS // 6):
                base = vector * 6
                field = [phi[source, plane, base + by_color(i)] for i in range(6)]
                upper = [phi[source, above, base + by_color(i)] for i in range(6)]
                lower = [phi[source, below, base + by_color(i)] for i in range(6)]
                total = [(1.0 - 6.0 * kappa_hop) * a for a in field]
                for terms in (
                    [last_x(a) for a in backward(plane, 0, field)],
                    [last_y(a) for a in backward(plane, 1, field)],
                    forward(plane, 2, upper),
                    backward(below, 2, lower),
                    forward(plane, 0, [next_x(a) for a in field]),
                    forward(plane, 1, [next_y(a) for a in field]),
                ):
                    total = [a + b for a, b in zip(total, terms)]
                for i in range(6):
                    phi[target, plane, base + by_color(i)] = total[i]
            return carry

        lax.fori_loop(0, PLANES, one, 0)

    for step in range(NSMEAR):
        one_step(step % 2, (step + 1) % 2)

    last = NSMEAR % 2
    for plane in range(PLANES):
        true_plane = z ^ plane
        for row in range(4):
            flat[true_plane, :, row * 128 : (row + 1) * 128] = phi[last, plane, :, 2 + row, :]
    out[...] = flat[...].reshape(PLANES * FIELDS, 512).astype(jnp.bfloat16)


def column_start(z, hop, side):
    slab = slab_of(z ^ hop, side)
    return pl.ds(pl.multiple_of(slab * 512, 512), 512)


def own_plane_kernel(*rest):
    blocks, out, column = rest[:PLANES], rest[PLANES], rest[PLANES + 1]
    z, h = my_place()
    for hop in range(PLANES):
        block = blocks[hop][...].astype(jnp.float32).reshape(PLANES, FIELDS, 512)
        column[:, :, column_start(z, hop, h)] = block
    out[...] = column[z].reshape(out.shape).astype(jnp.bfloat16)


FAR = 2


def reduce_sites(eigvecs, columns, sites, masks, vectors, sums):
    count = 4
    width = sites.shape[0]
    for group in range(eigvecs.shape[0] // (48 * count)):
        rows = eigvecs[group * 48 * count : (group + 1) * 48 * count, columns]
        product = lax.dot_general(
            rows, sites[...], (((1,), (1,)), ((), ())), preferred_element_type=jnp.float32
        ).reshape(count, 48, width)
        for part in range(2):
            sums[part, group * count : (group + 1) * count, :] = jnp.sum(
                product * masks[part][None], axis=1
            )
    return [
        lax.dot_general(
            vectors,
            sums[part],
            (((1,), (1,)), ((), ())),
            precision=lax.Precision.HIGHEST,
            preferred_element_type=jnp.float32,
        )[:4]
        for part in range(2)
    ]


def project_near_kernel(eigvecs, *rest):
    own, other = rest[:PLANES], list(rest[PLANES : 2 * PLANES - 1])
    coefficients, sites, sums = rest[2 * PLANES - 1 :]
    other.insert(FAR, None)
    half = PLANES * FIELDS
    z, h = my_place()
    for hop in range(PLANES):
        for blocks, side in ((own, h), (other, 1 - h)):
            rows = pl.ds(pl.multiple_of(side * half, half), half)
            here = jnp.zeros((half, 512), jnp.bfloat16) if blocks[hop] is None else blocks[hop][...]
            sites[rows, column_start(z, hop, side)] = here
    masks, vectors = projection_masks(2 * half, 0)
    parts = reduce_sites(eigvecs, slice(None), sites, masks, vectors, sums)
    for part in range(2):
        coefficients[4 * part : 4 * part + 4, :] = parts[part]


def project_far_kernel(eigvecs, near, block, coefficients, sums):
    z, h = my_place()
    masks, vectors = projection_masks(PLANES * FIELDS, 1 - h)
    parts = reduce_sites(eigvecs, column_start(z, FAR, 1 - h), block, masks, vectors, sums)
    for part in range(2):
        rows = slice(4 * part, 4 * part + 4)
        coefficients[rows, :] = near[rows, :] + parts[part]


def divided(a, by):
    return lax.shift_right_logical(a * (65536 // by + 1), 16)


def projection_masks(width, side):
    shape = (48, width)
    row = lax.broadcasted_iota(jnp.int32, shape, 0)
    column = lax.broadcasted_iota(jnp.int32, shape, 1)
    ri = lax.shift_right_logical(row + 8, 5)
    color = lax.shift_right_logical(row, 3) - 3 * ri
    pair = lax.shift_right_logical(column, 1)
    ri_right = column - 2 * pair
    vector = divided(pair, 3)
    color_right = pair - 3 * vector
    site_row = divided(column, FIELDS)
    site_row = 2 * (site_row & 3) + lax.shift_right_logical(site_row, 2) + side
    here = (color == color_right) & ((row & 7) == site_row)
    real = jnp.where(here & (ri == ri_right), 1.0, 0.0)
    imag = jnp.where(here & (ri != ri_right), jnp.where(ri == 0, 1.0, -1.0), 0.0)
    vectors = jnp.where((vector & 3)[:8] == lax.broadcasted_iota(jnp.int32, (8, shape[1]), 0), 1.0, 0.0)
    return (real, imag), vectors


def in_vmem(count):
    return [pl.BlockSpec(memory_space=pltpu.VMEM)] * count


def in_slabs(solutions, links, eigvecs):
    in_hbm = [pl.BlockSpec(memory_space=pltpu.HBM)]
    limit = pltpu.CompilerParams(vmem_limit_bytes=8 * 1024 * 1024)
    count = 2 * PLANES

    def swapped(block):
        return lax.ppermute(block, "space", [(i, i ^ 1) for i in range(count)])

    def across(block, hop):
        return lax.ppermute(block, "space", [(i, i ^ 2 * hop) for i in range(count)])

    far = solutions.reshape(FIELDS, 16, 128), links.reshape(LINKS, 16, 128)
    far = [pltpu.with_memory_space_constraint(array, pltpu.HBM) for array in far]
    ends, wide = pl.pallas_call(
        read_kernel,
        out_shape=[
            jax.ShapeDtypeStruct((4 * PARTS, 128), jnp.bfloat16),
            jax.ShapeDtypeStruct((PARTS, 16, 128), jnp.float32),
        ],
        in_specs=in_hbm * 2,
        out_specs=in_vmem(2),
        scratch_shapes=[
            pltpu.VMEM((4 * PARTS, 128), jnp.float32),
            pltpu.SemaphoreType.DMA(()),
            pltpu.SemaphoreType.DMA(()),
        ],
        compiler_params=pltpu.CompilerParams(vmem_limit_bytes=16 * 1024 * 1024),
        name="read",
    )(*far)
    packed = pl.pallas_call(
        pack_kernel,
        out_shape=[jax.ShapeDtypeStruct((WINDOW, 128), jnp.bfloat16)] * PLANES,
        in_specs=in_vmem(2),
        out_specs=in_vmem(PLANES),
        scratch_shapes=[
            pltpu.VMEM((PARTS, 8, 128), jnp.float32),
            pltpu.VMEM((PLANES, WINDOW, 128), jnp.bfloat16),
            pltpu.VMEM((4 * PARTS, 128), jnp.float32),
        ],
        compiler_params=limit,
        name="pack",
    )(wide, swapped(ends))
    vectors = eigvecs.shape[1]
    blocks = [packed[0]] + [across(packed[hop], hop) for hop in range(1, PLANES)]
    vectors = eigvecs.shape[1]
    block = pl.pallas_call(
        smear_kernel,
        out_shape=jax.ShapeDtypeStruct((PLANES * FIELDS, 512), jnp.bfloat16),
        in_specs=in_vmem(PLANES),
        out_specs=pl.BlockSpec(memory_space=pltpu.VMEM),
        scratch_shapes=[
            pltpu.VMEM((2, PLANES, FIELDS, 8, 128), jnp.float32),
            pltpu.VMEM((PLANES, LINKS, 8, 128), jnp.float32),
            pltpu.VMEM((PLANES, FIELDS, 512), jnp.float32),
        ],
        compiler_params=limit,
        cost_estimate=pl.CostEstimate(flops=10**9, bytes_accessed=2 * 10**7, transcendentals=0),
        name="smear",
    )(*blocks)
    own = [block] + [across(block, hop) for hop in range(1, PLANES)]
    own[FAR] = lax.optimization_barrier((own[FAR], own[1], own[3]))[0]
    other = [swapped(part) for part in own]
    smeared = pl.pallas_call(
        own_plane_kernel,
        out_shape=jax.ShapeDtypeStruct((FIELDS // 2, 2, 2048), jnp.bfloat16),
        in_specs=in_vmem(PLANES),
        out_specs=pl.BlockSpec(memory_space=pltpu.VMEM),
        scratch_shapes=[pltpu.VMEM((PLANES, FIELDS, 2048), jnp.float32)],
        compiler_params=limit,
        name="own_plane",
    )(*own)
    eigvecs = eigvecs.reshape(vectors * 48, 2048)
    near = pl.pallas_call(
        project_near_kernel,
        out_shape=jax.ShapeDtypeStruct((8, vectors), jnp.float32),
        in_specs=in_vmem(2 * PLANES),
        out_specs=pl.BlockSpec(memory_space=pltpu.VMEM),
        scratch_shapes=[
            pltpu.VMEM((2 * PLANES * FIELDS, 2048), jnp.bfloat16),
            pltpu.VMEM((2, vectors, 2 * PLANES * FIELDS), jnp.float32),
        ],
        compiler_params=limit,
        cost_estimate=pl.CostEstimate(flops=10**9, bytes_accessed=4 * 10**6, transcendentals=0),
        name="project_near",
    )(eigvecs, *own, *other[:FAR], *other[FAR + 1 :])
    coefficients = pl.pallas_call(
        project_far_kernel,
        out_shape=jax.ShapeDtypeStruct((8, vectors), jnp.float32),
        in_specs=in_vmem(3),
        out_specs=pl.BlockSpec(memory_space=pltpu.VMEM),
        scratch_shapes=[pltpu.VMEM((2, vectors, PLANES * FIELDS), jnp.float32)],
        compiler_params=limit,
        name="project_far",
    )(eigvecs, near, other[FAR])
    smeared = smeared.reshape(1, 4, 3, 2, 1, 2048).swapaxes(2, 3)
    return smeared, coefficients.T[None]


def local(solutions, links, eigvecs):
    fits = lax.axis_size("space") == 2 * PLANES and solutions.shape[:2] == (1, 4)
    fits = fits and solutions.shape[4:] == (1, 2048) and eigvecs.shape[1] % 4 == 0
    return (in_slabs if fits else by_planes)(solutions, links, eigvecs)


def solution(mesh):
    placed = (
        P(("cfg", "tm"), None, None, None, "space", None),
        P(("cfg", "tm"), None, None, None, None, "space", None),
        P(("cfg", "tm"), "space", None, None, None, None),
    )
    return jax.shard_map(
        local,
        mesh=mesh,
        in_specs=placed,
        out_specs=(
            P(("cfg", "tm"), None, None, None, "space", None),
            P(("cfg", "tm"), "space", None),
        ),
        check_vma=False,
    )
```

```python
import jax
import jax.numpy as jnp
from jax import lax
from jax.experimental import pallas as pl
from jax.experimental.pallas import tpu as pltpu
from jax.sharding import PartitionSpec as P

NSMEAR = 4
LX = 64


kappa_hop = 0.1


def swapped_2(block, axis, stride):
    count = lax.axis_size(axis)
    route = []
    for low in range(count):
        high = low | 1 << stride
        if high != low and high < count:
            route += [(low, high), (high, low)]
    return lax.ppermute(block, axis, route)


def for_sending(array):

    def short(part):
        return part.astype(jnp.bfloat16) if part.dtype == jnp.float32 else part

    return jax.tree.map(short, array)


def from_behind(block, axis, distance):
    devices = range(lax.axis_size(axis))
    route = [((i - distance) % len(devices), i) for i in devices]
    return lax.ppermute(block, axis, route)


def color_product(link_real, link_imag, field_real, field_imag):
    out_real = None
    out_imag = None
    for inner in range(3):
        column_real = link_real[:, None, :, inner]
        column_imag = link_imag[:, None, :, inner]
        entry_real = field_real[:, :, inner : inner + 1]
        entry_imag = field_imag[:, :, inner : inner + 1]
        term_real = column_real * entry_real - column_imag * entry_imag
        term_imag = column_real * entry_imag + column_imag * entry_real
        if out_real is None:
            out_real = term_real
            out_imag = term_imag
        else:
            out_real = out_real + term_real
            out_imag = out_imag + term_imag
    return (out_real, out_imag)


def adjoint_product(link_real, link_imag, field_real, field_imag):
    return color_product(
        jnp.swapaxes(link_real, 1, 2), -jnp.swapaxes(link_imag, 1, 2), field_real, field_imag
    )


def hopping(real, imag, link_flat):
    sites = real.shape[-1]
    x_place = lax.broadcasted_iota(jnp.int32, (sites,), 0) % LX
    at_end = x_place == LX - 1
    at_start = x_place == 0
    link_real = link_flat[:, 0, 0]
    link_imag = link_flat[:, 0, 1]
    next_real = jnp.where(at_end, jnp.roll(real, LX - 1, 3), jnp.roll(real, -1, 3))
    next_imag = jnp.where(at_end, jnp.roll(imag, LX - 1, 3), jnp.roll(imag, -1, 3))
    ahead_real, ahead_imag = color_product(link_real, link_imag, next_real, next_imag)
    back_real, back_imag = adjoint_product(link_real, link_imag, real, imag)
    total_real = ahead_real + jnp.where(
        at_start, jnp.roll(back_real, 1 - LX, 3), jnp.roll(back_real, 1, 3)
    )
    total_imag = ahead_imag + jnp.where(
        at_start, jnp.roll(back_imag, 1 - LX, 3), jnp.roll(back_imag, 1, 3)
    )
    link_real = link_flat[:, 1, 0]
    link_imag = link_flat[:, 1, 1]
    back_real, back_imag = adjoint_product(link_real, link_imag, real, imag)
    edge_rows = jnp.stack(
        [real[..., :LX], imag[..., :LX], back_real[..., sites - LX :], back_imag[..., sites - LX :]]
    )
    edges = swapped_2(edge_rows, "space", 0)
    next_real = jnp.concatenate([real[..., LX:], edges[0]], axis=3)
    next_imag = jnp.concatenate([imag[..., LX:], edges[1]], axis=3)
    ahead_real, ahead_imag = color_product(link_real, link_imag, next_real, next_imag)
    total_real = (
        total_real + ahead_real + jnp.concatenate([edges[2], back_real[..., : sites - LX]], axis=3)
    )
    total_imag = (
        total_imag + ahead_imag + jnp.concatenate([edges[3], back_imag[..., : sites - LX]], axis=3)
    )
    link_real = link_flat[:, 2, 0]
    link_imag = link_flat[:, 2, 1]
    upper = from_behind(for_sending(jnp.stack([real, imag])), "space", -2)
    ahead_real, ahead_imag = color_product(link_real, link_imag, upper[0], upper[1])
    back_real, back_imag = adjoint_product(link_real, link_imag, real, imag)
    lower = from_behind(for_sending(jnp.stack([back_real, back_imag])), "space", 2)
    total_real = total_real + ahead_real + lower[0]
    total_imag = total_imag + ahead_imag + lower[1]
    return (total_real, total_imag)


def pair_up(field):
    swapped = jnp.stack([field[:, :, 1], -field[:, :, 0]], axis=2)
    return jnp.concatenate([field, swapped], axis=1)


def project(left, right):
    left_flat = left.reshape(left.shape[0], left.shape[1], -1)
    right_flat = right.reshape(right.shape[0], right.shape[1], -1)
    return jnp.einsum("tkm,tvm->tkv", left_flat, right_flat, preferred_element_type=jnp.float32)


def by_planes(solutions, links, eigvecs):
    slices = solutions.shape[0]
    vectors = solutions.shape[1]
    real = solutions[:, :, 0].reshape(slices, vectors, 3, -1)
    imag = solutions[:, :, 1].reshape(slices, vectors, 3, -1)
    link_flat = links.reshape(links.shape[:5] + (-1,))
    for step in range(NSMEAR):
        hop_real, hop_imag = hopping(real, imag, link_flat)
        real = real + kappa_hop * (hop_real - 6.0 * real)
        imag = imag + kappa_hop * (hop_imag - 6.0 * imag)
    smeared = jnp.stack([real, imag], axis=2).reshape(solutions.shape).astype(jnp.bfloat16)
    coefficients = project(eigvecs, pair_up(lax.all_gather(smeared, "space", axis=4, tiled=True)))
    return (smeared, coefficients)


PLANES = 4
FIELDS = 24
LINKS = 54
PARTS = FIELDS + LINKS
WINDOW = PARTS * 8


def is_diagonal(part):
    return part >= FIELDS and (part - FIELDS) % 18 in (0, 4, 8)


def my_place():
    me = lax.axis_index("space")
    return me // 2, lax.rem(me, 2)


def slab_of(z, h):
    return jnp.where(h == 0, z, PLANES - 1 - z)


def read_kernel(field, link, ends, wide, narrow, field_done, link_done):
    field_copy = pltpu.make_async_copy(field, wide.at[:FIELDS], field_done)
    link_copy = pltpu.make_async_copy(link, wide.at[FIELDS:], link_done)
    field_copy.start()
    link_copy.start()
    field_copy.wait()
    link_copy.wait()
    for part in range(PARTS):
        if is_diagonal(part):
            wide[part] = wide[part] - 1.0
        narrow[4 * part : 4 * part + 2, :] = wide[part, 0:2, :]
        narrow[4 * part + 2 : 4 * part + 4, :] = wide[part, 14:16, :]
    ends[...] = narrow[...].astype(jnp.bfloat16)


def pack_kernel(wide, ends, *rest):
    outs, window, windows, narrow = rest[:PLANES], *rest[PLANES:]
    z, h = my_place()
    narrow[...] = ends[...].astype(jnp.float32)
    for slab in range(PLANES):
        low, high = max(4 * slab - 2, 0), min(4 * slab + 6, 16)
        to = low - (4 * slab - 2)
        window[:, to : to + high - low, :] = wide[:, low:high, :]
        for part in range(PARTS):
            if slab == 0:
                window[part, 0:2, :] = narrow[4 * part + 2 : 4 * part + 4, :]
            if slab == PLANES - 1:
                window[part, 6:8, :] = narrow[4 * part : 4 * part + 2, :]
        windows[slab] = window[...].reshape(WINDOW, 128).astype(jnp.bfloat16)
    for hop in range(PLANES):
        outs[hop][...] = windows[slab_of(z ^ hop, h)]


def by_color(part):
    vector, rest = part // 6, part % 6
    return vector * 6 + rest % 3 * 2 + rest // 3


def apply_links(entry, sign, field):
    reals = []
    imags = []
    for row in range(3):
        real = imag = None
        for inner in range(3):
            re, im = entry(row, inner)
            real_a, real_b = re * field[inner], im * field[3 + inner]
            imag_a, imag_b = re * field[3 + inner], im * field[inner]
            if sign > 0:
                term_real, term_imag = real_a - real_b, imag_a + imag_b
            else:
                term_real, term_imag = real_a + real_b, imag_a - imag_b
            real = term_real if real is None else real + term_real
            imag = term_imag if imag is None else imag + term_imag
        reals.append(real)
        imags.append(imag)
    return reals + imags


def smear_kernel(*rest):
    blocks, (out, phi, links, flat) = rest[:PLANES], rest[PLANES:]
    lane = lax.broadcasted_iota(jnp.int32, (8, 128), 1)
    x_place = lane % LX
    at_end = x_place == LX - 1
    at_start = x_place == 0
    low = lane < LX

    z, _ = my_place()
    up = 1 + 2 * lax.rem(z, 2)

    def scaled(part, value):
        return kappa_hop * (value + 1.0 if is_diagonal(part) else value)

    for plane in range(PLANES):
        values = blocks[plane][...].astype(jnp.float32).reshape(PARTS, 8, 128)
        for part in range(FIELDS):
            phi[0, plane, by_color(part)] = values[part]
        for part in range(FIELDS, PARTS):
            links[plane, part - FIELDS] = scaled(part, values[part])

    def next_x(a):
        return jnp.where(at_end, pltpu.roll(a, LX - 1, 1), pltpu.roll(a, 127, 1))

    def last_x(a):
        return jnp.where(at_start, pltpu.roll(a, LX + 1, 1), pltpu.roll(a, 1, 1))

    def next_y(a):
        other = pltpu.roll(a, LX, 1)
        return jnp.where(low, other, pltpu.roll(other, 7, 0))

    def last_y(a):
        other = pltpu.roll(a, LX, 1)
        return jnp.where(low, pltpu.roll(other, 1, 0), other)

    def forward(plane, along, field):
        def entry(row, inner):
            at = along * 18 + row * 3 + inner
            return links[plane, at], links[plane, at + 9]

        return apply_links(entry, 1, field)

    def backward(plane, along, field):
        def entry(row, inner):
            at = along * 18 + inner * 3 + row
            return links[plane, at], links[plane, at + 9]

        return apply_links(entry, -1, field)

    def one_step(source, target):
        def one(plane, carry):
            above = lax.rem(plane + up, PLANES)
            below = lax.rem(plane + PLANES - up, PLANES)
            for vector in range(FIELDS // 6):
                base = vector * 6
                field = [phi[source, plane, base + by_color(i)] for i in range(6)]
                upper = [phi[source, above, base + by_color(i)] for i in range(6)]
                lower = [phi[source, below, base + by_color(i)] for i in range(6)]
                total = [(1.0 - 6.0 * kappa_hop) * a for a in field]
                for terms in (
                    [last_x(a) for a in backward(plane, 0, field)],
                    [last_y(a) for a in backward(plane, 1, field)],
                    forward(plane, 2, upper),
                    backward(below, 2, lower),
                    forward(plane, 0, [next_x(a) for a in field]),
                    forward(plane, 1, [next_y(a) for a in field]),
                ):
                    total = [a + b for a, b in zip(total, terms)]
                for i in range(6):
                    phi[target, plane, base + by_color(i)] = total[i]
            return carry

        lax.fori_loop(0, PLANES, one, 0)

    for step in range(NSMEAR):
        one_step(step % 2, (step + 1) % 2)

    last = NSMEAR % 2
    for plane in range(PLANES):
        true_plane = z ^ plane
        for row in range(4):
            flat[true_plane, :, row * 128 : (row + 1) * 128] = phi[last, plane, :, 2 + row, :]
    out[...] = flat[...].reshape(PLANES * FIELDS, 512).astype(jnp.bfloat16)


def column_start(z, hop, side):
    slab = slab_of(z ^ hop, side)
    return pl.ds(pl.multiple_of(slab * 512, 512), 512)


def own_plane_kernel(*rest):
    blocks, out, column = rest[:PLANES], rest[PLANES], rest[PLANES + 1]
    z, h = my_place()
    for hop in range(PLANES):
        block = blocks[hop][...].astype(jnp.float32).reshape(PLANES, FIELDS, 512)
        column[:, :, column_start(z, hop, h)] = block
    out[...] = column[z].reshape(out.shape).astype(jnp.bfloat16)


NEAR = (0, 1)
FAR = (2, 3)


def reduce_sites(eigvecs, pieces, masks, vectors, sums):
    count = 4
    for group in range(eigvecs.shape[0] // (48 * count)):
        rows = slice(group * 48 * count, (group + 1) * 48 * count)
        product = None
        for columns, sites in pieces:
            term = lax.dot_general(
                eigvecs[rows, columns],
                sites[...],
                (((1,), (1,)), ((), ())),
                preferred_element_type=jnp.float32,
            )
            product = term if product is None else product + term
        product = product.reshape(count, 48, product.shape[1])
        for part in range(2):
            sums[part, group * count : (group + 1) * count, :] = jnp.sum(
                product * masks[part][None], axis=1
            )
    return [
        lax.dot_general(
            vectors,
            sums[part],
            (((1,), (1,)), ((), ())),
            precision=lax.Precision.HIGHEST,
            preferred_element_type=jnp.float32,
        )[:4]
        for part in range(2)
    ]


def project_near_kernel(eigvecs, *rest):
    own, other = rest[:PLANES], dict(zip(NEAR, rest[PLANES:]))
    coefficients, sites, sums = rest[PLANES + len(NEAR) :]
    half = PLANES * FIELDS
    z, h = my_place()
    for hop in range(PLANES):
        rows = pl.ds(pl.multiple_of(h * half, half), half)
        sites[rows, column_start(z, hop, h)] = own[hop][...]
        rows = pl.ds(pl.multiple_of((1 - h) * half, half), half)
        here = other[hop][...] if hop in NEAR else jnp.zeros((half, 512), jnp.bfloat16)
        sites[rows, column_start(z, hop, 1 - h)] = here
    masks, vectors = projection_masks(2 * half, 0)
    parts = reduce_sites(eigvecs, [(slice(None), sites)], masks, vectors, sums)
    for part in range(2):
        coefficients[4 * part : 4 * part + 4, :] = parts[part]


def project_far_kernel(eigvecs, near, *rest):
    blocks, (coefficients, sums) = rest[: len(FAR)], rest[len(FAR) :]
    z, h = my_place()
    masks, vectors = projection_masks(PLANES * FIELDS, 1 - h)
    pieces = [(column_start(z, hop, 1 - h), block) for hop, block in zip(FAR, blocks)]
    parts = reduce_sites(eigvecs, pieces, masks, vectors, sums)
    for part in range(2):
        rows = slice(4 * part, 4 * part + 4)
        coefficients[rows, :] = near[rows, :] + parts[part]


def divided(a, by):
    return lax.shift_right_logical(a * (65536 // by + 1), 16)


def projection_masks(width, side):
    shape = (48, width)
    row = lax.broadcasted_iota(jnp.int32, shape, 0)
    column = lax.broadcasted_iota(jnp.int32, shape, 1)
    ri = lax.shift_right_logical(row + 8, 5)
    color = lax.shift_right_logical(row, 3) - 3 * ri
    pair = lax.shift_right_logical(column, 1)
    ri_right = column - 2 * pair
    vector = divided(pair, 3)
    color_right = pair - 3 * vector
    site_row = divided(column, FIELDS)
    site_row = 2 * (site_row & 3) + lax.shift_right_logical(site_row, 2) + side
    here = (color == color_right) & ((row & 7) == site_row)
    real = jnp.where(here & (ri == ri_right), 1.0, 0.0)
    imag = jnp.where(here & (ri != ri_right), jnp.where(ri == 0, 1.0, -1.0), 0.0)
    vectors = jnp.where((vector & 3)[:8] == lax.broadcasted_iota(jnp.int32, (8, shape[1]), 0), 1.0, 0.0)
    return (real, imag), vectors


def in_vmem(count):
    return [pl.BlockSpec(memory_space=pltpu.VMEM)] * count


def in_slabs(solutions, links, eigvecs):
    in_hbm = [pl.BlockSpec(memory_space=pltpu.HBM)]
    limit = pltpu.CompilerParams(vmem_limit_bytes=8 * 1024 * 1024)
    count = 2 * PLANES

    def swapped(block):
        return lax.ppermute(block, "space", [(i, i ^ 1) for i in range(count)])

    def across(block, hop):
        return lax.ppermute(block, "space", [(i, i ^ 2 * hop) for i in range(count)])

    far = solutions.reshape(FIELDS, 16, 128), links.reshape(LINKS, 16, 128)
    far = [pltpu.with_memory_space_constraint(array, pltpu.HBM) for array in far]
    ends, wide = pl.pallas_call(
        read_kernel,
        out_shape=[
            jax.ShapeDtypeStruct((4 * PARTS, 128), jnp.bfloat16),
            jax.ShapeDtypeStruct((PARTS, 16, 128), jnp.float32),
        ],
        in_specs=in_hbm * 2,
        out_specs=in_vmem(2),
        scratch_shapes=[
            pltpu.VMEM((4 * PARTS, 128), jnp.float32),
            pltpu.SemaphoreType.DMA(()),
            pltpu.SemaphoreType.DMA(()),
        ],
        compiler_params=pltpu.CompilerParams(vmem_limit_bytes=16 * 1024 * 1024),
        name="read",
    )(*far)
    packed = pl.pallas_call(
        pack_kernel,
        out_shape=[jax.ShapeDtypeStruct((WINDOW, 128), jnp.bfloat16)] * PLANES,
        in_specs=in_vmem(2),
        out_specs=in_vmem(PLANES),
        scratch_shapes=[
            pltpu.VMEM((PARTS, 8, 128), jnp.float32),
            pltpu.VMEM((PLANES, WINDOW, 128), jnp.bfloat16),
            pltpu.VMEM((4 * PARTS, 128), jnp.float32),
        ],
        compiler_params=limit,
        name="pack",
    )(wide, swapped(ends))
    vectors = eigvecs.shape[1]
    blocks = [packed[0]] + [across(packed[hop], hop) for hop in range(1, PLANES)]
    vectors = eigvecs.shape[1]
    block = pl.pallas_call(
        smear_kernel,
        out_shape=jax.ShapeDtypeStruct((PLANES * FIELDS, 512), jnp.bfloat16),
        in_specs=in_vmem(PLANES),
        out_specs=pl.BlockSpec(memory_space=pltpu.VMEM),
        scratch_shapes=[
            pltpu.VMEM((2, PLANES, FIELDS, 8, 128), jnp.float32),
            pltpu.VMEM((PLANES, LINKS, 8, 128), jnp.float32),
            pltpu.VMEM((PLANES, FIELDS, 512), jnp.float32),
        ],
        compiler_params=limit,
        cost_estimate=pl.CostEstimate(flops=10**9, bytes_accessed=2 * 10**7, transcendentals=0),
        name="smear",
    )(*blocks)
    own = [block, across(block, 1), across(block, 2)]
    own.append(across(own[2], 1))
    other = [swapped(part) for part in own[:2]]
    other.append(swapped(lax.optimization_barrier((own[2], other[0]))[0]))
    other.append(swapped(own[3]))
    smeared = pl.pallas_call(
        own_plane_kernel,
        out_shape=jax.ShapeDtypeStruct((FIELDS // 2, 2, 2048), jnp.bfloat16),
        in_specs=in_vmem(PLANES),
        out_specs=pl.BlockSpec(memory_space=pltpu.VMEM),
        scratch_shapes=[pltpu.VMEM((PLANES, FIELDS, 2048), jnp.float32)],
        compiler_params=limit,
        name="own_plane",
    )(*own)
    eigvecs = eigvecs.reshape(vectors * 48, 2048)
    near = pl.pallas_call(
        project_near_kernel,
        out_shape=jax.ShapeDtypeStruct((8, vectors), jnp.float32),
        in_specs=in_vmem(1 + PLANES + len(NEAR)),
        out_specs=pl.BlockSpec(memory_space=pltpu.VMEM),
        scratch_shapes=[
            pltpu.VMEM((2 * PLANES * FIELDS, 2048), jnp.bfloat16),
            pltpu.VMEM((2, vectors, 2 * PLANES * FIELDS), jnp.float32),
        ],
        compiler_params=limit,
        cost_estimate=pl.CostEstimate(flops=10**9, bytes_accessed=4 * 10**6, transcendentals=0),
        name="project_near",
    )(eigvecs, *own, *[other[hop] for hop in NEAR])
    coefficients = pl.pallas_call(
        project_far_kernel,
        out_shape=jax.ShapeDtypeStruct((8, vectors), jnp.float32),
        in_specs=in_vmem(2 + len(FAR)),
        out_specs=pl.BlockSpec(memory_space=pltpu.VMEM),
        scratch_shapes=[pltpu.VMEM((2, vectors, PLANES * FIELDS), jnp.float32)],
        compiler_params=limit,
        name="project_far",
    )(eigvecs, near, *[other[hop] for hop in FAR])
    smeared = smeared.reshape(1, 4, 3, 2, 1, 2048).swapaxes(2, 3)
    return smeared, coefficients.T[None]


def local(solutions, links, eigvecs):
    fits = lax.axis_size("space") == 2 * PLANES and solutions.shape[:2] == (1, 4)
    fits = fits and solutions.shape[4:] == (1, 2048) and eigvecs.shape[1] % 4 == 0
    return (in_slabs if fits else by_planes)(solutions, links, eigvecs)


def solution(mesh):
    placed = (
        P(("cfg", "tm"), None, None, None, "space", None),
        P(("cfg", "tm"), None, None, None, None, "space", None),
        P(("cfg", "tm"), "space", None, None, None, None),
    )
    return jax.shard_map(
        local,
        mesh=mesh,
        in_specs=placed,
        out_specs=(
            P(("cfg", "tm"), None, None, None, "space", None),
            P(("cfg", "tm"), "space", None),
        ),
        check_vma=False,
    )
```

```python
import jax
import jax.numpy as jnp
from jax import lax
from jax.experimental import pallas as pl
from jax.experimental.pallas import tpu as pltpu
from jax.sharding import PartitionSpec as P

NSMEAR = 4
LX = 64


kappa_hop = 0.1


def swapped_2(block, axis, stride):
    count = lax.axis_size(axis)
    route = []
    for low in range(count):
        high = low | 1 << stride
        if high != low and high < count:
            route += [(low, high), (high, low)]
    return lax.ppermute(block, axis, route)


def for_sending(array):

    def short(part):
        return part.astype(jnp.bfloat16) if part.dtype == jnp.float32 else part

    return jax.tree.map(short, array)


def from_behind(block, axis, distance):
    devices = range(lax.axis_size(axis))
    route = [((i - distance) % len(devices), i) for i in devices]
    return lax.ppermute(block, axis, route)


def color_product(link_real, link_imag, field_real, field_imag):
    out_real = None
    out_imag = None
    for inner in range(3):
        column_real = link_real[:, None, :, inner]
        column_imag = link_imag[:, None, :, inner]
        entry_real = field_real[:, :, inner : inner + 1]
        entry_imag = field_imag[:, :, inner : inner + 1]
        term_real = column_real * entry_real - column_imag * entry_imag
        term_imag = column_real * entry_imag + column_imag * entry_real
        if out_real is None:
            out_real = term_real
            out_imag = term_imag
        else:
            out_real = out_real + term_real
            out_imag = out_imag + term_imag
    return (out_real, out_imag)


def adjoint_product(link_real, link_imag, field_real, field_imag):
    return color_product(
        jnp.swapaxes(link_real, 1, 2), -jnp.swapaxes(link_imag, 1, 2), field_real, field_imag
    )


def hopping(real, imag, link_flat):
    sites = real.shape[-1]
    x_place = lax.broadcasted_iota(jnp.int32, (sites,), 0) % LX
    at_end = x_place == LX - 1
    at_start = x_place == 0
    link_real = link_flat[:, 0, 0]
    link_imag = link_flat[:, 0, 1]
    next_real = jnp.where(at_end, jnp.roll(real, LX - 1, 3), jnp.roll(real, -1, 3))
    next_imag = jnp.where(at_end, jnp.roll(imag, LX - 1, 3), jnp.roll(imag, -1, 3))
    ahead_real, ahead_imag = color_product(link_real, link_imag, next_real, next_imag)
    back_real, back_imag = adjoint_product(link_real, link_imag, real, imag)
    total_real = ahead_real + jnp.where(
        at_start, jnp.roll(back_real, 1 - LX, 3), jnp.roll(back_real, 1, 3)
    )
    total_imag = ahead_imag + jnp.where(
        at_start, jnp.roll(back_imag, 1 - LX, 3), jnp.roll(back_imag, 1, 3)
    )
    link_real = link_flat[:, 1, 0]
    link_imag = link_flat[:, 1, 1]
    back_real, back_imag = adjoint_product(link_real, link_imag, real, imag)
    edge_rows = jnp.stack(
        [real[..., :LX], imag[..., :LX], back_real[..., sites - LX :], back_imag[..., sites - LX :]]
    )
    edges = swapped_2(edge_rows, "space", 0)
    next_real = jnp.concatenate([real[..., LX:], edges[0]], axis=3)
    next_imag = jnp.concatenate([imag[..., LX:], edges[1]], axis=3)
    ahead_real, ahead_imag = color_product(link_real, link_imag, next_real, next_imag)
    total_real = (
        total_real + ahead_real + jnp.concatenate([edges[2], back_real[..., : sites - LX]], axis=3)
    )
    total_imag = (
        total_imag + ahead_imag + jnp.concatenate([edges[3], back_imag[..., : sites - LX]], axis=3)
    )
    link_real = link_flat[:, 2, 0]
    link_imag = link_flat[:, 2, 1]
    upper = from_behind(for_sending(jnp.stack([real, imag])), "space", -2)
    ahead_real, ahead_imag = color_product(link_real, link_imag, upper[0], upper[1])
    back_real, back_imag = adjoint_product(link_real, link_imag, real, imag)
    lower = from_behind(for_sending(jnp.stack([back_real, back_imag])), "space", 2)
    total_real = total_real + ahead_real + lower[0]
    total_imag = total_imag + ahead_imag + lower[1]
    return (total_real, total_imag)


def pair_up(field):
    swapped = jnp.stack([field[:, :, 1], -field[:, :, 0]], axis=2)
    return jnp.concatenate([field, swapped], axis=1)


def project(left, right):
    left_flat = left.reshape(left.shape[0], left.shape[1], -1)
    right_flat = right.reshape(right.shape[0], right.shape[1], -1)
    return jnp.einsum("tkm,tvm->tkv", left_flat, right_flat, preferred_element_type=jnp.float32)


def by_planes(solutions, links, eigvecs):
    slices = solutions.shape[0]
    vectors = solutions.shape[1]
    real = solutions[:, :, 0].reshape(slices, vectors, 3, -1)
    imag = solutions[:, :, 1].reshape(slices, vectors, 3, -1)
    link_flat = links.reshape(links.shape[:5] + (-1,))
    for step in range(NSMEAR):
        hop_real, hop_imag = hopping(real, imag, link_flat)
        real = real + kappa_hop * (hop_real - 6.0 * real)
        imag = imag + kappa_hop * (hop_imag - 6.0 * imag)
    smeared = jnp.stack([real, imag], axis=2).reshape(solutions.shape).astype(jnp.bfloat16)
    coefficients = project(eigvecs, pair_up(lax.all_gather(smeared, "space", axis=4, tiled=True)))
    return (smeared, coefficients)


PLANES = 4
FIELDS = 24
LINKS = 54
PARTS = FIELDS + LINKS
WINDOW = PARTS * 8


def is_diagonal(part):
    return part >= FIELDS and (part - FIELDS) % 18 in (0, 4, 8)


def my_place():
    me = lax.axis_index("space")
    return me // 2, lax.rem(me, 2)


def slab_of(z, h):
    return jnp.where(h == 0, z, PLANES - 1 - z)


def read_kernel(field, link, ends, wide, narrow, field_done, link_done):
    field_copy = pltpu.make_async_copy(field, wide.at[:FIELDS], field_done)
    link_copy = pltpu.make_async_copy(link, wide.at[FIELDS:], link_done)
    field_copy.start()
    link_copy.start()
    field_copy.wait()
    link_copy.wait()
    for part in range(PARTS):
        if is_diagonal(part):
            wide[part] = wide[part] - 1.0
        narrow[4 * part : 4 * part + 2, :] = wide[part, 0:2, :]
        narrow[4 * part + 2 : 4 * part + 4, :] = wide[part, 14:16, :]
    ends[...] = narrow[...].astype(jnp.bfloat16)


def pack_kernel(wide, ends, *rest):
    outs, window, windows, narrow = rest[:PLANES], *rest[PLANES:]
    z, h = my_place()
    narrow[...] = ends[...].astype(jnp.float32)
    for slab in range(PLANES):
        low, high = max(4 * slab - 2, 0), min(4 * slab + 6, 16)
        to = low - (4 * slab - 2)
        window[:, to : to + high - low, :] = wide[:, low:high, :]
        for part in range(PARTS):
            if slab == 0:
                window[part, 0:2, :] = narrow[4 * part + 2 : 4 * part + 4, :]
            if slab == PLANES - 1:
                window[part, 6:8, :] = narrow[4 * part : 4 * part + 2, :]
        windows[slab] = window[...].reshape(WINDOW, 128).astype(jnp.bfloat16)
    for hop in range(PLANES):
        outs[hop][...] = windows[slab_of(z ^ hop, h)]


def by_color(part):
    vector, rest = part // 6, part % 6
    return vector * 6 + rest % 3 * 2 + rest // 3


def apply_links(entry, sign, field):
    reals = []
    imags = []
    for row in range(3):
        real = imag = None
        for inner in range(3):
            re, im = entry(row, inner)
            real_a, real_b = re * field[inner], im * field[3 + inner]
            imag_a, imag_b = re * field[3 + inner], im * field[inner]
            if sign > 0:
                term_real, term_imag = real_a - real_b, imag_a + imag_b
            else:
                term_real, term_imag = real_a + real_b, imag_a - imag_b
            real = term_real if real is None else real + term_real
            imag = term_imag if imag is None else imag + term_imag
        reals.append(real)
        imags.append(imag)
    return reals + imags


def smear_kernel(*rest):
    blocks, (out, phi, links, flat) = rest[:PLANES], rest[PLANES:]
    lane = lax.broadcasted_iota(jnp.int32, (8, 128), 1)
    x_place = lane % LX
    at_end = x_place == LX - 1
    at_start = x_place == 0
    low = lane < LX

    z, _ = my_place()
    up = 1 + 2 * lax.rem(z, 2)

    def scaled(part, value):
        return kappa_hop * (value + 1.0 if is_diagonal(part) else value)

    for plane in range(PLANES):
        values = blocks[plane][...].astype(jnp.float32).reshape(PARTS, 8, 128)
        for part in range(FIELDS):
            phi[0, plane, by_color(part)] = values[part]
        for part in range(FIELDS, PARTS):
            links[plane, part - FIELDS] = scaled(part, values[part])

    def next_x(a):
        return jnp.where(at_end, pltpu.roll(a, LX - 1, 1), pltpu.roll(a, 127, 1))

    def last_x(a):
        return jnp.where(at_start, pltpu.roll(a, LX + 1, 1), pltpu.roll(a, 1, 1))

    def next_y(a):
        other = pltpu.roll(a, LX, 1)
        return jnp.where(low, other, pltpu.roll(other, 7, 0))

    def last_y(a):
        other = pltpu.roll(a, LX, 1)
        return jnp.where(low, pltpu.roll(other, 1, 0), other)

    def forward(plane, along, field):
        def entry(row, inner):
            at = along * 18 + row * 3 + inner
            return links[plane, at], links[plane, at + 9]

        return apply_links(entry, 1, field)

    def backward(plane, along, field):
        def entry(row, inner):
            at = along * 18 + inner * 3 + row
            return links[plane, at], links[plane, at + 9]

        return apply_links(entry, -1, field)

    def one_step(source, target):
        def one(plane, carry):
            above = lax.rem(plane + up, PLANES)
            below = lax.rem(plane + PLANES - up, PLANES)
            for vector in range(FIELDS // 6):
                base = vector * 6
                field = [phi[source, plane, base + by_color(i)] for i in range(6)]
                upper = [phi[source, above, base + by_color(i)] for i in range(6)]
                lower = [phi[source, below, base + by_color(i)] for i in range(6)]
                total = [(1.0 - 6.0 * kappa_hop) * a for a in field]
                for terms in (
                    [last_x(a) for a in backward(plane, 0, field)],
                    [last_y(a) for a in backward(plane, 1, field)],
                    forward(plane, 2, upper),
                    backward(below, 2, lower),
                    forward(plane, 0, [next_x(a) for a in field]),
                    forward(plane, 1, [next_y(a) for a in field]),
                ):
                    total = [a + b for a, b in zip(total, terms)]
                for i in range(6):
                    phi[target, plane, base + by_color(i)] = total[i]
            return carry

        lax.fori_loop(0, PLANES, one, 0)

    for step in range(NSMEAR):
        one_step(step % 2, (step + 1) % 2)

    last = NSMEAR % 2
    for plane in range(PLANES):
        true_plane = z ^ plane
        for row in range(4):
            flat[true_plane, :, row * 128 : (row + 1) * 128] = phi[last, plane, :, 2 + row, :]
    out[...] = flat[...].reshape(PLANES * FIELDS, 512).astype(jnp.bfloat16)


def column_start(z, hop, side):
    slab = slab_of(z ^ hop, side)
    return pl.ds(pl.multiple_of(slab * 512, 512), 512)


def own_plane_kernel(*rest):
    blocks, out, column = rest[:PLANES], rest[PLANES], rest[PLANES + 1]
    z, h = my_place()
    for hop in range(PLANES):
        block = blocks[hop][...].astype(jnp.float32).reshape(PLANES, FIELDS, 512)
        column[:, :, column_start(z, hop, h)] = block
    out[...] = column[z].reshape(out.shape).astype(jnp.bfloat16)


NEAR = (0, 1)
FAR = (2, 3)


def reduce_sites(eigvecs, pieces, masks, vectors, sums):
    count = 8
    for group in range(eigvecs.shape[0] // (48 * count)):
        rows = slice(group * 48 * count, (group + 1) * 48 * count)
        product = None
        for columns, sites in pieces:
            term = lax.dot_general(
                eigvecs[rows, columns],
                sites[...],
                (((1,), (1,)), ((), ())),
                preferred_element_type=jnp.float32,
            )
            product = term if product is None else product + term
        product = product.reshape(count, 48, product.shape[1])
        for part in range(2):
            sums[part, group * count : (group + 1) * count, :] = jnp.sum(
                product * masks[part][None], axis=1
            )
    return [
        lax.dot_general(
            vectors,
            sums[part],
            (((1,), (1,)), ((), ())),
            precision=lax.Precision.HIGHEST,
            preferred_element_type=jnp.float32,
        )[:4]
        for part in range(2)
    ]


def project_near_kernel(eigvecs, *rest):
    own, other = rest[:PLANES], dict(zip(NEAR, rest[PLANES:]))
    coefficients, sites, sums = rest[PLANES + len(NEAR) :]
    half = PLANES * FIELDS
    z, h = my_place()
    for hop in range(PLANES):
        rows = pl.ds(pl.multiple_of(h * half, half), half)
        sites[rows, column_start(z, hop, h)] = own[hop][...]
        rows = pl.ds(pl.multiple_of((1 - h) * half, half), half)
        here = other[hop][...] if hop in NEAR else jnp.zeros((half, 512), jnp.bfloat16)
        sites[rows, column_start(z, hop, 1 - h)] = here
    masks, vectors = projection_masks(2 * half, 0)
    parts = reduce_sites(eigvecs, [(slice(None), sites)], masks, vectors, sums)
    for part in range(2):
        coefficients[4 * part : 4 * part + 4, :] = parts[part]


def project_far_kernel(eigvecs, near, *rest):
    blocks, (coefficients, sums) = rest[: len(FAR)], rest[len(FAR) :]
    z, h = my_place()
    masks, vectors = projection_masks(PLANES * FIELDS, 1 - h)
    pieces = [(column_start(z, hop, 1 - h), block) for hop, block in zip(FAR, blocks)]
    parts = reduce_sites(eigvecs, pieces, masks, vectors, sums)
    for part in range(2):
        rows = slice(4 * part, 4 * part + 4)
        coefficients[rows, :] = near[rows, :] + parts[part]


def divided(a, by):
    return lax.shift_right_logical(a * (65536 // by + 1), 16)


def projection_masks(width, side):
    shape = (48, width)
    row = lax.broadcasted_iota(jnp.int32, shape, 0)
    column = lax.broadcasted_iota(jnp.int32, shape, 1)
    ri = lax.shift_right_logical(row + 8, 5)
    color = lax.shift_right_logical(row, 3) - 3 * ri
    pair = lax.shift_right_logical(column, 1)
    ri_right = column - 2 * pair
    vector = divided(pair, 3)
    color_right = pair - 3 * vector
    site_row = divided(column, FIELDS)
    site_row = 2 * (site_row & 3) + lax.shift_right_logical(site_row, 2) + side
    here = (color == color_right) & ((row & 7) == site_row)
    real = jnp.where(here & (ri == ri_right), 1.0, 0.0)
    imag = jnp.where(here & (ri != ri_right), jnp.where(ri == 0, 1.0, -1.0), 0.0)
    vectors = jnp.where((vector & 3)[:8] == lax.broadcasted_iota(jnp.int32, (8, shape[1]), 0), 1.0, 0.0)
    return (real, imag), vectors


def in_vmem(count):
    return [pl.BlockSpec(memory_space=pltpu.VMEM)] * count


def in_slabs(solutions, links, eigvecs):
    in_hbm = [pl.BlockSpec(memory_space=pltpu.HBM)]
    limit = pltpu.CompilerParams(vmem_limit_bytes=8 * 1024 * 1024)
    count = 2 * PLANES

    def swapped(block):
        return lax.ppermute(block, "space", [(i, i ^ 1) for i in range(count)])

    def across(block, hop):
        return lax.ppermute(block, "space", [(i, i ^ 2 * hop) for i in range(count)])

    far = solutions.reshape(FIELDS, 16, 128), links.reshape(LINKS, 16, 128)
    far = [pltpu.with_memory_space_constraint(array, pltpu.HBM) for array in far]
    ends, wide = pl.pallas_call(
        read_kernel,
        out_shape=[
            jax.ShapeDtypeStruct((4 * PARTS, 128), jnp.bfloat16),
            jax.ShapeDtypeStruct((PARTS, 16, 128), jnp.float32),
        ],
        in_specs=in_hbm * 2,
        out_specs=in_vmem(2),
        scratch_shapes=[
            pltpu.VMEM((4 * PARTS, 128), jnp.float32),
            pltpu.SemaphoreType.DMA(()),
            pltpu.SemaphoreType.DMA(()),
        ],
        compiler_params=pltpu.CompilerParams(vmem_limit_bytes=16 * 1024 * 1024),
        name="read",
    )(*far)
    packed = pl.pallas_call(
        pack_kernel,
        out_shape=[jax.ShapeDtypeStruct((WINDOW, 128), jnp.bfloat16)] * PLANES,
        in_specs=in_vmem(2),
        out_specs=in_vmem(PLANES),
        scratch_shapes=[
            pltpu.VMEM((PARTS, 8, 128), jnp.float32),
            pltpu.VMEM((PLANES, WINDOW, 128), jnp.bfloat16),
            pltpu.VMEM((4 * PARTS, 128), jnp.float32),
        ],
        compiler_params=limit,
        name="pack",
    )(wide, swapped(ends))
    vectors = eigvecs.shape[1]
    blocks = [packed[0]] + [across(packed[hop], hop) for hop in range(1, PLANES)]
    vectors = eigvecs.shape[1]
    block = pl.pallas_call(
        smear_kernel,
        out_shape=jax.ShapeDtypeStruct((PLANES * FIELDS, 512), jnp.bfloat16),
        in_specs=in_vmem(PLANES),
        out_specs=pl.BlockSpec(memory_space=pltpu.VMEM),
        scratch_shapes=[
            pltpu.VMEM((2, PLANES, FIELDS, 8, 128), jnp.float32),
            pltpu.VMEM((PLANES, LINKS, 8, 128), jnp.float32),
            pltpu.VMEM((PLANES, FIELDS, 512), jnp.float32),
        ],
        compiler_params=limit,
        cost_estimate=pl.CostEstimate(flops=10**9, bytes_accessed=2 * 10**7, transcendentals=0),
        name="smear",
    )(*blocks)
    own = [block, across(block, 1), across(block, 2)]
    own.append(across(own[2], 1))
    other = [swapped(part) for part in own[:2]]
    other.append(swapped(lax.optimization_barrier((own[2], other[0]))[0]))
    other.append(swapped(own[3]))
    smeared = pl.pallas_call(
        own_plane_kernel,
        out_shape=jax.ShapeDtypeStruct((FIELDS // 2, 2, 2048), jnp.bfloat16),
        in_specs=in_vmem(PLANES),
        out_specs=pl.BlockSpec(memory_space=pltpu.VMEM),
        scratch_shapes=[pltpu.VMEM((PLANES, FIELDS, 2048), jnp.float32)],
        compiler_params=limit,
        name="own_plane",
    )(*own)
    eigvecs = eigvecs.reshape(vectors * 48, 2048)
    near = pl.pallas_call(
        project_near_kernel,
        out_shape=jax.ShapeDtypeStruct((8, vectors), jnp.float32),
        in_specs=in_vmem(1 + PLANES + len(NEAR)),
        out_specs=pl.BlockSpec(memory_space=pltpu.VMEM),
        scratch_shapes=[
            pltpu.VMEM((2 * PLANES * FIELDS, 2048), jnp.bfloat16),
            pltpu.VMEM((2, vectors, 2 * PLANES * FIELDS), jnp.float32),
        ],
        compiler_params=limit,
        cost_estimate=pl.CostEstimate(flops=10**9, bytes_accessed=4 * 10**6, transcendentals=0),
        name="project_near",
    )(eigvecs, *own, *[other[hop] for hop in NEAR])
    coefficients = pl.pallas_call(
        project_far_kernel,
        out_shape=jax.ShapeDtypeStruct((8, vectors), jnp.float32),
        in_specs=in_vmem(2 + len(FAR)),
        out_specs=pl.BlockSpec(memory_space=pltpu.VMEM),
        scratch_shapes=[pltpu.VMEM((2, vectors, PLANES * FIELDS), jnp.float32)],
        compiler_params=limit,
        name="project_far",
    )(eigvecs, near, *[other[hop] for hop in FAR])
    smeared = smeared.reshape(1, 4, 3, 2, 1, 2048).swapaxes(2, 3)
    return smeared, coefficients.T[None]


def local(solutions, links, eigvecs):
    fits = lax.axis_size("space") == 2 * PLANES and solutions.shape[:2] == (1, 4)
    fits = fits and solutions.shape[4:] == (1, 2048) and eigvecs.shape[1] % 8 == 0
    return (in_slabs if fits else by_planes)(solutions, links, eigvecs)


def solution(mesh):
    placed = (
        P(("cfg", "tm"), None, None, None, "space", None),
        P(("cfg", "tm"), None, None, None, None, "space", None),
        P(("cfg", "tm"), "space", None, None, None, None),
    )
    return jax.shard_map(
        local,
        mesh=mesh,
        in_specs=placed,
        out_specs=(
            P(("cfg", "tm"), None, None, None, "space", None),
            P(("cfg", "tm"), "space", None),
        ),
        check_vma=False,
    )
```
